32 devices in a mesh: au: 8 (over z, core), ia: 4 (over y, x).
Axes of the slice: x: 2, y: 2, z: 4, core: 2. Of those that a mesh axis runs over, the one named last changes fastest.
Arguments:
- user_emb: float32 [4096, 512], P('au'), may hold values from -6 to 6
- item_emb: float32 [8192, 512], P(('ia', 'au')), may hold values from -6 to 6
- tiles: bfloat16 [8, 48, 256, 256], P('au', 'ia'), may hold values from -0.15625 to 0.15625
- block_rows: int32 [8, 48], P('au', 'ia'), may hold values from 0 to 1
- block_cols: int32 [8, 48], P('au', 'ia'), may hold values from 0 to 7
- block_counts: int32 [8, 4], P('au', 'ia'), may hold values from 1 to 12, as said below
- w_self: float32 [512, 512], replicated, may hold values from -0.25 to 0.25
- w_inter: float32 [512, 512], replicated, may hold values from -0.25 to 0.25
Outputs:
- new_users: float32 [4096, 512], P(('au', 'ia'))
- new_items: float32 [8192, 512], P(('ia', 'au'))
The draws below stay inside these ranges and needn't reach their ends.
Inputs may be any that keep to these rules, and one draw needn't show every extreme that they name: `block_counts`: slots at or after a device's count hold no block; within one device's first count slots the (row, column) pairs are distinct; some device lists 12 blocks.
All inputs are finite; a program needn't handle non-finite values.
Results may differ from the reference program's by a relative error of at most 0.0037.
Values may be sent and summed in bfloat16 or wider, within the bound.
No kernel may reach another device: no remote copies, remote signals or barrier semaphores. Data moves between devices by JAX's collectives and lax.ppermute only.
A program may use at most 64 MiB of HBM per device.

```python
import jax
import jax.numpy as jnp
from jax import lax

D = 512
BS = 256
UROWS = 512
ICOLS = 2048
MAXB = 12
USERS = 4096
ITEMS = 8192
N_AU = 8
N_IA = 4


def layout_pairs(key):
    keys = jax.random.split(jax.random.fold_in(key, 7), N_AU * N_IA)
    places = UROWS // BS * (ICOLS // BS)
    perms = jax.vmap(lambda single: jax.random.permutation(single, places))(keys)[:, :MAXB]
    perms = perms.astype(jnp.int32)
    rows = (perms // (ICOLS // BS)).reshape(N_AU, N_IA * MAXB)
    cols = (perms % (ICOLS // BS)).reshape(N_AU, N_IA * MAXB)
    return (rows, cols)


def draw_block_rows(key, part):
    return layout_pairs(key)[0]


def draw_block_cols(key, part):
    return layout_pairs(key)[1]


def draw_block_counts(key, part):
    counts = jax.random.randint(jax.random.fold_in(key, 11), (N_AU * N_IA,), 1, MAXB + 1)
    fullest = jax.random.randint(jax.random.fold_in(key, 13), (), 0, N_AU * N_IA)
    counts = jnp.where(jnp.arange(N_AU * N_IA) == fullest, MAXB, counts)
    return counts.astype(jnp.int32).reshape(N_AU, N_IA)


def steps_of(stream_key, extent, shards, smallest, largest):
    factor_of, own = 1.0, jax.random.fold_in(stream_key, 6)
    for axis_at, parts in shards:
        steps = jnp.exp(jax.random.uniform(jax.random.fold_in(own, axis_at), (parts,), jnp.float32, smallest / len(shards), largest / len(shards)))
        factor_of = factor_of * jnp.repeat(steps, extent[axis_at] // parts).reshape([-1 if axis == axis_at else 1 for axis in range(len(extent))])
    return factor_of


def centred(own_key, shape, spread, reach, cuts=(), held_as=jnp.bfloat16):
    loudness = steps_of(own_key, shape, cuts, -0.22, 0.18) if cuts else 1.0
    entries = jax.random.normal(own_key, shape, jnp.float32) * spread * loudness
    return jnp.minimum(jnp.maximum(entries, -reach), reach).astype(held_as)


def setup_inputs(seed: int = 0) -> dict:
    key_of = jax.random.split(jax.random.key(seed), 9)
    return {
        "user_emb": centred(key_of[0], (USERS, D), 1.0, 6.0, ((0, 8),), jnp.float32),
        "item_emb": centred(key_of[1], (ITEMS, D), 1.0, 6.0, ((0, 32),), jnp.float32),
        "tiles": centred(key_of[2], (N_AU, N_IA * MAXB, BS, BS), (BS * MAXB // 2) ** -0.5, 0.15625, ((0, 8), (1, 4))),
        "block_rows": draw_block_rows(jax.random.fold_in(key_of[8], 71), 0),
        "block_cols": draw_block_cols(jax.random.fold_in(key_of[8], 71), 0),
        "block_counts": draw_block_counts(jax.random.fold_in(key_of[8], 71), 0),
        "w_self": centred(key_of[6], (D, D), D ** -0.5, 0.25, (), jnp.float32),
        "w_inter": centred(key_of[7], (D, D), D ** -0.5, 0.25, (), jnp.float32),
    }


def update(side, emb, w_self, w_inter):
    mixed = jnp.dot(side + emb, w_self, precision=lax.Precision.HIGHEST, preferred_element_type=jnp.float32)
    mixed = mixed + jnp.dot(side * emb, w_inter, precision=lax.Precision.HIGHEST, preferred_element_type=jnp.float32)
    return jax.nn.leaky_relu(mixed, 0.2)


def reference(user_emb, item_emb, tiles, block_rows, block_cols, block_counts, w_self, w_inter):
    row_blocks = UROWS // BS
    col_blocks = ICOLS // BS
    slot_ids = jnp.arange(N_IA * MAXB, dtype=jnp.int32)
    owner = slot_ids // MAXB
    within = slot_ids % MAXB
    item_half = item_emb.astype(jnp.bfloat16).reshape(N_IA, col_blocks, BS, D)

    def user_side(index):
        valid = (within < block_counts[index][owner]).astype(jnp.float32)
        blocks = item_half[owner, block_cols[index]]
        contrib = jnp.einsum("kij,kjd->kid", tiles[index].astype(jnp.float32), blocks.astype(jnp.float32))
        select = (block_rows[index][:, None] == jnp.arange(row_blocks, dtype=jnp.int32)[None, :]).astype(jnp.float32)
        select = select * valid[:, None]
        return jnp.einsum("kr,kid->rid", select, contrib).reshape(UROWS, D)

    sides = lax.map(user_side, jnp.arange(N_AU, dtype=jnp.int32))
    new_users = update(sides.reshape(USERS, D), user_emb, w_self, w_inter)
    user_half = new_users.astype(jnp.bfloat16).reshape(N_AU, row_blocks, BS, D)

    def item_step(total, index):
        valid = (within < block_counts[index][owner]).astype(jnp.float32)
        blocks = user_half[index][block_rows[index]]
        contrib = jnp.einsum("kij,kid->kjd", tiles[index].astype(jnp.float32), blocks.astype(jnp.float32))
        target = owner * col_blocks + block_cols[index]
        select = (target[:, None] == jnp.arange(N_IA * col_blocks, dtype=jnp.int32)[None, :]).astype(jnp.float32)
        select = select * valid[:, None]
        return total + jnp.einsum("kc,kjd->cjd", select, contrib), None

    start = jnp.zeros((N_IA * col_blocks, BS, D), jnp.float32)
    total, unused = lax.scan(item_step, start, jnp.arange(N_AU, dtype=jnp.int32))
    new_items = update(total.reshape(ITEMS, D), item_emb, w_self, w_inter)
    return new_users, new_items
```

```python
import functools

import jax
import jax.numpy as jnp
from jax import lax
from jax.experimental import pallas as pl
from jax.experimental.pallas import tpu as pltpu
from jax.sharding import PartitionSpec as P

F32 = jnp.float32
BF16 = jnp.bfloat16
VMEM = pl.BlockSpec(memory_space=pltpu.VMEM)
SMEM = pl.BlockSpec(memory_space=pltpu.SMEM)
PARAMS = pltpu.CompilerParams(vmem_limit_bytes=40 * 1024 * 1024)


def call(kernel, out_shape, in_specs, flops=0, nbytes=0, scratch=()):
    return pl.pallas_call(
        kernel,
        out_shape=out_shape,
        in_specs=in_specs,
        out_specs=jax.tree.map(lambda _: VMEM, out_shape),
        scratch_shapes=scratch,
        compiler_params=PARAMS,
        cost_estimate=pl.CostEstimate(flops=flops, bytes_accessed=nbytes, transcendentals=0),
    )


def shape(*dims, dtype=BF16):
    return jax.ShapeDtypeStruct(dims, dtype)


def split(x):
    hi = x.astype(BF16)
    return hi, (x - hi.astype(F32)).astype(BF16)


def dot(a, b):
    return jnp.dot(a, b, preferred_element_type=F32)


def prepare(piece, direct, rows, cols, count, tiles, user_emb, w_self, w_inter, adj, adj_t, w_hi, w_lo, own):
    me_au = lax.axis_index("au") if direct[0] else 0
    me_ia = lax.axis_index("ia") if direct[1] else 0
    edge = tiles.shape[2]
    depth = w_self.shape[0]
    adj[...] = jnp.zeros_like(adj)
    adj_t[...] = jnp.zeros_like(adj_t)

    def place(slot, carry):
        col = pl.multiple_of((cols[0, slot] ^ me_au) * edge, edge)
        for part in range(edge // piece):
            at = (rows[0, slot] * (edge // piece) + part) ^ me_ia
            row = pl.multiple_of(at * piece, piece)
            block = tiles[0, slot, part * piece : (part + 1) * piece, :]
            adj[pl.ds(row, piece), pl.ds(col, edge)] = block
            adj_t[pl.ds(col, edge), pl.ds(row, piece)] = block.T
        return carry

    lax.fori_loop(0, count[0, 0], place, 0)
    for k, w in enumerate((w_self, w_inter)):
        w_hi[k * depth : (k + 1) * depth, :], w_lo[k * depth : (k + 1) * depth, :] = split(w[...])
    height = own.shape[0]
    own[...] = user_emb[pl.ds(pl.multiple_of(lax.axis_index("ia") * height, height), height), :]


def user_sums(n, adj, *refs):
    blocks, outs = refs[:n], refs[n:]
    total = None
    at = 0
    for block in blocks:
        term = dot(adj[:, at : at + block.shape[0]], block[...])
        total = term if total is None else total + term
        at += block.shape[0]
    height = outs[0].shape[0]
    for k, out in enumerate(outs):
        out[...] = total[k * height : (k + 1) * height].astype(out.dtype)


def item_sums(n, adj_t, *refs):
    shares, outs = refs[:n], refs[n:]
    users = jnp.concatenate([share[...] for share in shares], axis=0)
    height = outs[0].shape[0]
    for k, out in enumerate(outs):
        out[...] = dot(adj_t[k * height : (k + 1) * height, :], users).astype(out.dtype)


def update(n, emb, w_hi, w_lo, *refs):
    parts, outs = refs[:n], refs[n:]
    side = parts[0][...].astype(F32)
    for part in parts[1:]:
        side = side + part[...].astype(F32)
    own = emb[...]
    hi, lo = split(jnp.concatenate([side + own, side * own], axis=1))
    mixed = dot(hi, w_lo[...]) + dot(lo, w_hi[...]) + dot(hi, w_hi[...])
    mixed = jnp.where(mixed >= 0, mixed, 0.2 * mixed)
    for out in outs:
        out[...] = mixed.astype(out.dtype)


def chip_sums(n, *refs):
    mine, theirs, outs = refs[:n], refs[n : 2 * n], refs[2 * n :]
    for a, b, out in zip(mine, theirs, outs):
        out[...] = (a[...] + b[...].astype(F32)).astype(out.dtype)


def local(n_au, n_ia, user_emb, item_emb, tiles, block_rows, block_cols, block_counts, w_self, w_inter):
    edge = tiles.shape[2]
    depth = w_self.shape[0]
    users, held = user_emb.shape[0], item_emb.shape[0]
    items = held * n_au
    share = users // n_ia
    direct = (n_au == 8 and held == edge, n_ia == 4 and edge % share == 0)

    def swap(x, axis, n, by):
        return lax.ppermute(x, axis, [(i, i ^ by) for i in range(n)])

    item_half = item_emb.astype(BF16)
    if direct[0]:
        blocks = [None] * 8
        blocks[0] = item_half
        for k in (2, 4, 6):
            blocks[k] = swap(item_half, "au", 8, k)
        for k in (0, 2, 4, 6):
            blocks[k + 1] = swap(blocks[k], "au", 8, 1)
    else:
        blocks = [lax.all_gather(item_half, "au", axis=0, tiled=True)]

    adj, adj_t, w_hi, w_lo, own_emb = call(
        functools.partial(prepare, share if direct[1] else edge, direct),
        (shape(users, items), shape(items, users), shape(2 * depth, depth), shape(2 * depth, depth), shape(share, depth, dtype=F32)),
        [SMEM, SMEM, SMEM, VMEM, VMEM, VMEM, VMEM],
        nbytes=10 << 20,
    )(block_rows, block_cols, block_counts, tiles, user_emb, w_self, w_inter)

    work = 2 * users * items * depth
    if direct[1]:
        shares = (shape(share, depth, dtype=F32),) + (shape(share, depth),) * (n_ia - 1)
        sums = call(functools.partial(user_sums, len(blocks)), shares, [VMEM] * (1 + len(blocks)), work, 6 << 20)(adj, *blocks)
        sums = [sums[0]] + [swap(sums[k], "ia", n_ia, k) for k in range(1, n_ia)]
    else:
        (sums,) = call(functools.partial(user_sums, len(blocks)), (shape(users, depth, dtype=F32),), [VMEM] * (1 + len(blocks)), work, 6 << 20)(adj, *blocks)
        sums = [lax.psum_scatter(sums, "ia", scatter_dimension=0, tiled=True)]
    new_users, user_half = call(
        functools.partial(update, len(sums)),
        (shape(share, depth, dtype=F32), shape(share, depth)),
        [VMEM] * (3 + len(sums)),
        12 * share * depth * depth,
        3 << 20,
    )(own_emb, w_hi, w_lo, *sums)

    if direct[1]:
        halves = [user_half] + [swap(user_half, "ia", n_ia, k) for k in range(1, n_ia)]
    else:
        halves = [lax.all_gather(user_half, "ia", axis=0, tiled=True)]
    if direct[0]:
        shares = tuple(shape(held, depth, dtype=BF16 if k % 2 else F32) for k in range(8))
        sums = call(functools.partial(item_sums, len(halves)), shares, [VMEM] * (1 + len(halves)), work, 6 << 20)(adj_t, *halves)
        theirs = [swap(sums[k], "au", 8, 1) for k in (1, 3, 5, 7)]
        shares = (shape(held, depth, dtype=F32),) + (shape(held, depth),) * 3
        sums = call(functools.partial(chip_sums, 4), shares, [VMEM] * 8, 0, 6 << 20)(*sums[0::2], *theirs)
        sums = [sums[0]] + [swap(sums[k], "au", 8, 2 * k) for k in (1, 2, 3)]
    else:
        (sums,) = call(functools.partial(item_sums, len(halves)), (shape(items, depth, dtype=F32),), [VMEM] * (1 + len(halves)), work, 6 << 20)(adj_t, *halves)
        sums = [lax.psum_scatter(sums, "au", scatter_dimension=0, tiled=True)]
    (new_items,) = call(
        functools.partial(update, len(sums)),
        (shape(held, depth, dtype=F32),),
        [VMEM] * (3 + len(sums)),
        12 * held * depth * depth,
        4 << 20,
    )(item_emb, w_hi, w_lo, *sums)
    return (new_users, new_items)


def solution(mesh):
    in_specs = (
        P("au", None),
        P(("ia", "au"), None),
        P("au", "ia", None, None),
        P("au", "ia"),
        P("au", "ia"),
        P("au", "ia"),
        P(),
        P(),
    )
    out_specs = (P(("au", "ia"), None), P(("ia", "au"), None))
    return jax.shard_map(
        functools.partial(local, mesh.shape["au"], mesh.shape["ia"]),
        mesh=mesh,
        in_specs=in_specs,
        out_specs=out_specs,
        check_vma=False,
    )
```

```python
import functools

import jax
import jax.numpy as jnp
from jax import lax
from jax.experimental import pallas as pl
from jax.experimental.pallas import tpu as pltpu
from jax.sharding import PartitionSpec as P

F32 = jnp.float32
BF16 = jnp.bfloat16
VMEM = pl.BlockSpec(memory_space=pltpu.VMEM)
SMEM = pl.BlockSpec(memory_space=pltpu.SMEM)
PARAMS = pltpu.CompilerParams(vmem_limit_bytes=40 * 1024 * 1024)


def call(kernel, out_shape, in_specs, flops=0, nbytes=0, scratch=()):
    return pl.pallas_call(
        kernel,
        out_shape=out_shape,
        in_specs=in_specs,
        out_specs=jax.tree.map(lambda _: VMEM, out_shape),
        scratch_shapes=scratch,
        compiler_params=PARAMS,
        cost_estimate=pl.CostEstimate(flops=flops, bytes_accessed=nbytes, transcendentals=0),
    )


def shape(*dims, dtype=BF16):
    return jax.ShapeDtypeStruct(dims, dtype)


def split(x):
    hi = x.astype(BF16)
    return hi, (x - hi.astype(F32)).astype(BF16)


def dot(a, b):
    return jnp.dot(a, b, preferred_element_type=F32)


def dense(piece, direct, rows, cols, count, item_half, tiles, adj, adj_t, again):
    me_au = lax.axis_index("au") if direct[0] else 0
    me_ia = lax.axis_index("ia") if direct[1] else 0
    edge = tiles.shape[2]
    again[...] = item_half[...]
    adj[...] = jnp.zeros_like(adj)
    adj_t[...] = jnp.zeros_like(adj_t)

    def place(slot, carry):
        at = cols[0, slot]
        if direct[0]:
            at = slot_of(me_au, at)
        col = pl.multiple_of(at * edge, edge)
        for part in range(edge // piece):
            at = (rows[0, slot] * (edge // piece) + part) ^ me_ia
            row = pl.multiple_of(at * piece, piece)
            block = tiles[0, slot, part * piece : (part + 1) * piece, :]
            adj[pl.ds(row, piece), pl.ds(col, edge)] = block
            adj_t[pl.ds(col, edge), pl.ds(row, piece)] = block.T
        return carry

    lax.fori_loop(0, count[0, 0], place, 0)


def halves_of(item_half, user_emb, w_self, w_inter, w_hi, w_lo, own, again):
    depth = w_self.shape[0]
    again[...] = item_half[...]
    for k, w in enumerate((w_self, w_inter)):
        w_hi[k * depth : (k + 1) * depth, :], w_lo[k * depth : (k + 1) * depth, :] = split(w[...])
    height = own.shape[0]
    own[...] = user_emb[pl.ds(pl.multiple_of(lax.axis_index("ia") * height, height), height), :]


def slot_of(me, block):
    apart = block ^ me
    z, turn = me >> 1, apart >> 1
    swapped = ((z == 1) | (z == 2)) & ((turn == 1) | (turn == 2))
    return jnp.where(swapped, 3 - turn, turn) * 2 + (apart & 1)


TURN_1 = ((0, 2), (3, 1), (1, 0), (2, 3))
TURN_2 = ((0, 1), (3, 2), (1, 3), (2, 0))
MIDDLE = ((1, 2), (2, 1))
ENDS = ((2, 3), (1, 0))


def back(pairs):
    return tuple((b, a) for a, b in pairs)


def send(x, pairs):
    return lax.ppermute(x, "au", [(2 * a + core, 2 * b + core) for a, b in pairs for core in (0, 1)])


def user_sums(sizes, adj, *refs):
    blocks, outs = refs[: sum(sizes)], refs[sum(sizes) :]
    total = None
    at = first = 0
    for size in sizes:
        block = sum((ref[...] for ref in blocks[first + 1 : first + size]), blocks[first][...])
        term = dot(adj[:, at : at + block.shape[0]], block)
        total = term if total is None else total + term
        at += block.shape[0]
        first += size
    height = outs[0].shape[0]
    for k, out in enumerate(outs):
        out[...] = total[k * height : (k + 1) * height].astype(out.dtype)


def item_sums(n, adj_t, *refs):
    shares, outs = refs[:n], refs[n:]
    users = jnp.concatenate([share[...] for share in shares], axis=0)
    height = outs[0].shape[0]
    for k, out in enumerate(outs):
        out[...] = dot(adj_t[k * height : (k + 1) * height, :], users).astype(out.dtype)


def update(n, emb, w_hi, w_lo, *refs):
    parts, outs = refs[:n], refs[n:]
    side = parts[0][...].astype(F32)
    for part in parts[1:]:
        side = side + part[...].astype(F32)
    own = emb[...]
    hi, lo = split(jnp.concatenate([side + own, side * own], axis=1))
    mixed = dot(hi, w_lo[...]) + dot(lo, w_hi[...]) + dot(hi, w_hi[...])
    mixed = jnp.where(mixed >= 0, mixed, 0.2 * mixed)
    for out in outs:
        out[...] = mixed.astype(out.dtype)


def chip_sums(n, *refs):
    mine, theirs, outs = refs[:n], refs[n : 2 * n], refs[2 * n :]
    for a, b, out in zip(mine, theirs, outs):
        out[...] = (a[...].astype(F32) + b[...].astype(F32)).astype(out.dtype)


def local(n_au, n_ia, user_emb, item_emb, tiles, block_rows, block_cols, block_counts, w_self, w_inter):
    edge = tiles.shape[2]
    depth = w_self.shape[0]
    users, held = user_emb.shape[0], item_emb.shape[0]
    items = held * n_au
    share = users // n_ia
    direct = (n_au == 8 and held == edge, n_ia == 4 and edge % share == 0)

    def swap(x, axis, n, by):
        return lax.ppermute(x, axis, [(i, i ^ by) for i in range(n)])

    item_half = item_emb.astype(BF16)
    if direct[0]:
        first = send(item_half, TURN_1)

    adj, adj_t, again = call(
        functools.partial(dense, share if direct[1] else edge, direct),
        (shape(users, items), shape(items, users), shape(held, depth)),
        [SMEM, SMEM, SMEM, VMEM, VMEM],
        nbytes=8 << 20,
    )(block_rows, block_cols, block_counts, item_half, tiles)
    w_hi, w_lo, own_emb, later = call(
        halves_of,
        (shape(2 * depth, depth), shape(2 * depth, depth), shape(share, depth, dtype=F32), shape(held, depth)),
        [VMEM] * 4,
        nbytes=5 << 20,
    )(again, user_emb, w_self, w_inter)
    if direct[0]:
        second = send(again, TURN_2)
        middle = send(later, MIDDLE)
        ends = send(first, ENDS)
        groups = ((item_half,), (first,), (second,), (middle, ends))
        groups = tuple(g for group in groups for g in (group, tuple(swap(x, "au", 8, 1) for x in group)))
    else:
        groups = ((lax.all_gather(item_half, "au", axis=0, tiled=True),),)
    blocks = [x for group in groups for x in group]
    sizes = tuple(len(group) for group in groups)

    work = 2 * users * items * depth
    if direct[1]:
        shares = (shape(share, depth, dtype=F32),) + (shape(share, depth),) * (n_ia - 1)
        sums = call(functools.partial(user_sums, sizes), shares, [VMEM] * (1 + len(blocks)), work, 6 << 20)(adj, *blocks)
        sums = [sums[0]] + [swap(sums[k], "ia", n_ia, k) for k in range(1, n_ia)]
    else:
        (sums,) = call(functools.partial(user_sums, sizes), (shape(users, depth, dtype=F32),), [VMEM] * (1 + len(blocks)), work, 6 << 20)(adj, *blocks)
        sums = [lax.psum_scatter(sums, "ia", scatter_dimension=0, tiled=True)]
    new_users, user_half = call(
        functools.partial(update, len(sums)),
        (shape(share, depth, dtype=F32), shape(share, depth)),
        [VMEM] * (3 + len(sums)),
        12 * share * depth * depth,
        3 << 20,
    )(own_emb, w_hi, w_lo, *sums)

    if direct[1]:
        halves = [user_half] + [swap(user_half, "ia", n_ia, k) for k in range(1, n_ia)]
    else:
        halves = [lax.all_gather(user_half, "ia", axis=0, tiled=True)]
    if direct[0]:
        shares = tuple(shape(held, depth, dtype=BF16 if k % 2 else F32) for k in range(8))
        sums = call(functools.partial(item_sums, len(halves)), shares, [VMEM] * (1 + len(halves)), work, 6 << 20)(adj_t, *halves)
        theirs = [swap(sums[k], "au", 8, 1) for k in (1, 3, 5, 7)]
        shares = (shape(held, depth, dtype=F32),) + (shape(held, depth),) * 3
        sums = call(functools.partial(chip_sums, 4), shares, [VMEM] * 8, 0, 6 << 20)(*sums[0::2], *theirs)
        handed = send(sums[3], back(ENDS))
        arrived = [send(sums[2], back(TURN_2)), send(sums[3], back(MIDDLE))]
        (onward,) = call(functools.partial(chip_sums, 1), (shape(held, depth),), [VMEM] * 2, 0, 1 << 20)(sums[1], handed)
        sums = [sums[0], send(onward, back(TURN_1))] + arrived
    else:
        (sums,) = call(functools.partial(item_sums, len(halves)), (shape(items, depth, dtype=F32),), [VMEM] * (1 + len(halves)), work, 6 << 20)(adj_t, *halves)
        sums = [lax.psum_scatter(sums, "au", scatter_dimension=0, tiled=True)]
    (new_items,) = call(
        functools.partial(update, len(sums)),
        (shape(held, depth, dtype=F32),),
        [VMEM] * (3 + len(sums)),
        12 * held * depth * depth,
        4 << 20,
    )(item_emb, w_hi, w_lo, *sums)
    return (new_users, new_items)


def solution(mesh):
    in_specs = (
        P("au", None),
        P(("ia", "au"), None),
        P("au", "ia", None, None),
        P("au", "ia"),
        P("au", "ia"),
        P("au", "ia"),
        P(),
        P(),
    )
    out_specs = (P(("au", "ia"), None), P(("ia", "au"), None))
    return jax.shard_map(
        functools.partial(local, mesh.shape["au"], mesh.shape["ia"]),
        mesh=mesh,
        in_specs=in_specs,
        out_specs=out_specs,
        check_vma=False,
    )
```

```python
import functools

import jax
import jax.numpy as jnp
from jax import lax
from jax.experimental import pallas as pl
from jax.experimental.pallas import tpu as pltpu
from jax.sharding import PartitionSpec as P

F32 = jnp.float32
BF16 = jnp.bfloat16
VMEM = pl.BlockSpec(memory_space=pltpu.VMEM)
SMEM = pl.BlockSpec(memory_space=pltpu.SMEM)
PARAMS = pltpu.CompilerParams(vmem_limit_bytes=40 * 1024 * 1024)

TURN_1 = ((0, 2), (3, 1), (1, 0), (2, 3))
TURN_2 = ((0, 1), (3, 2), (1, 3), (2, 0))
MIDDLE = ((1, 2), (2, 1), (0, 0), (3, 3))
HANDED = ((2, 3), (1, 0), (3, 2), (0, 1))


def back(pairs):
    return tuple((b, a) for a, b in pairs)


def send(x, pairs):
    return lax.ppermute(x, "au", [(2 * a + core, 2 * b + core) for a, b in pairs for core in (0, 1)])


def swap(x, axis, n, by):
    return lax.ppermute(x, axis, [(i, i ^ by) for i in range(n)])


def slot_of(me, block):
    apart = block ^ me
    turn = apart >> 1
    swapped = in_middle() & ((turn == 1) | (turn == 2))
    return jnp.where(swapped, 3 - turn, turn) * 2 + (apart & 1)


def in_middle():
    z = lax.axis_index("au") >> 1
    return (z == 1) | (z == 2)


def call(kernel, out_shape, operands, smem=0, flops=0, nbytes=0):
    return pl.pallas_call(
        kernel,
        out_shape=out_shape,
        in_specs=[SMEM] * smem + [VMEM] * (len(operands) - smem),
        out_specs=jax.tree.map(lambda _: VMEM, out_shape),
        compiler_params=PARAMS,
        cost_estimate=pl.CostEstimate(flops=flops, bytes_accessed=nbytes, transcendentals=0),
    )(*operands)


def shape(*dims, dtype=BF16):
    return jax.ShapeDtypeStruct(dims, dtype)


def split(x):
    hi = x.astype(BF16)
    return hi, (x - hi.astype(F32)).astype(BF16)


def dot(a, b):
    return jnp.dot(a, b, preferred_element_type=F32)


def total(refs):
    value = refs[0][...].astype(F32)
    for ref in refs[1:]:
        value = value + ref[...].astype(F32)
    return value


def dense(piece, turns, rows, cols, count, tiles, adj):
    edge = tiles.shape[2]
    adj[...] = jnp.zeros_like(adj)

    def place(slot, carry):
        at = cols[0, slot]
        if turns:
            at = slot_of(lax.axis_index("au"), at)
        col = pl.multiple_of(at * edge, edge)
        for part in range(edge // piece):
            row = rows[0, slot] * (edge // piece) + part
            if turns:
                row = row ^ lax.axis_index("ia")
            row = pl.multiple_of(row * piece, piece)
            adj[pl.ds(row, piece), pl.ds(col, edge)] = tiles[0, slot, part * piece : (part + 1) * piece, :]
        return carry

    lax.fori_loop(0, count[0, 0], place, 0)


def flip(edge, adj, *outs):
    n = len(outs)
    for k in range(adj.shape[1] // edge):
        out = outs[k % n]
        out[k // n * edge : (k // n + 1) * edge, :] = adj[:, k * edge : (k + 1) * edge].T


def ready(edge, adj, user_emb, w_self, w_inter, w_hi, w_lo, own, *adj_t):
    weights(user_emb, w_self, w_inter, w_hi, w_lo, own)
    flip(edge, adj, *adj_t)


def weights(user_emb, w_self, w_inter, w_hi, w_lo, own):
    depth = w_self.shape[0]
    for k, w in enumerate((w_self, w_inter)):
        w_hi[k * depth : (k + 1) * depth, :], w_lo[k * depth : (k + 1) * depth, :] = split(w[...])
    height = own.shape[0]
    own[...] = user_emb[pl.ds(pl.multiple_of(lax.axis_index("ia") * height, height), height), :]


def block_sums(adj, first, blocks):
    edge = blocks[0].shape[0]
    return sum(dot(adj[:, (first + k) * edge : (first + k + 1) * edge], block) for k, block in enumerate(blocks))


def early_sums(adj, *refs):
    *blocks, sums = refs
    sums[...] = block_sums(adj, 0, [block[...] for block in blocks])


def late_sums(adj, early, second, second_other, middle, ends, middle_other, ends_other, *outs):
    inner = in_middle()
    blocks = [second[...], second_other[...]]
    blocks += [jnp.where(inner, a[...], b[...]) for a, b in ((middle, ends), (middle_other, ends_other))]
    sums = early[...] + block_sums(adj, 4, blocks)
    height = outs[0].shape[0]
    for k, out in enumerate(outs):
        out[...] = sums[k * height : (k + 1) * height].astype(out.dtype)


def user_sums(adj, items, out):
    out[...] = dot(adj[...], items[...])


def item_sums(slots, n, *refs):
    adj_t, shares, outs = refs[:2], refs[2 : 2 + 2 * n], refs[-len(slots) :]
    users = [jnp.concatenate([share[...] for share in shares[core * n : core * n + n]], axis=0) for core in (0, 1)]
    edge = outs[0].shape[0]
    for slot, out in zip(slots, outs):
        rows = slice(slot * edge, (slot + 1) * edge)
        out[...] = (dot(adj_t[0][rows, :], users[0]) + dot(adj_t[1][rows, :], users[1])).astype(out.dtype)


def all_sums(adj_t, users, out):
    out[...] = dot(adj_t[...], users[...])


def pass_on(sums, handed, out):
    given = jnp.where(in_middle(), handed[...].astype(F32), 0)
    out[...] = (sums[...] + given).astype(out.dtype)


def update(n, emb, w_hi, w_lo, *refs, inner=0):
    parts, outs = refs[:n], refs[n:]
    side = total(parts[inner:])
    if inner:
        side = side + jnp.where(in_middle(), total(parts[:inner]), 0)
    own = emb[...]
    height = own.shape[0]
    hi, lo = split(jnp.concatenate([side + own, side * own], axis=1))
    both = dot(jnp.concatenate([hi, lo], axis=0), w_hi[...])
    mixed = both[:height] + (both[height:] + dot(hi, w_lo[...]))
    mixed = jnp.where(mixed >= 0, mixed, 0.2 * mixed)
    for out in outs:
        out[...] = mixed.astype(out.dtype)


def in_turns(user_emb, item_emb, tiles, block_rows, block_cols, block_counts, w_self, w_inter):
    depth = w_self.shape[0]
    users, held = user_emb.shape[0], item_emb.shape[0]
    items = held * 8
    share = users // 4
    work = 2 * users * items * depth

    def other(x):
        return swap(x, "au", 8, 1)

    def after(x, *done):
        return lax.optimization_barrier((x, *done))[0]

    mine = item_emb.astype(BF16)
    first = send(mine, TURN_1)
    (adj,) = call(
        functools.partial(dense, share, True),
        (shape(users, items),),
        (block_rows, block_cols, block_counts, tiles),
        smem=3,
        nbytes=8 << 20,
    )
    second = send(after(mine, adj), TURN_2)
    w_hi, w_lo, own_emb, adj_t, others_t = call(
        functools.partial(ready, held),
        (shape(2 * depth, depth), shape(2 * depth, depth), shape(share, depth, dtype=F32))
        + (shape(items // 2, users), shape(items // 2, users)),
        (adj, user_emb, w_self, w_inter),
        nbytes=9 << 20,
    )
    middle = send(after(mine, w_hi), MIDDLE)
    first = after(first, w_hi)
    ends = send(first, HANDED)
    (early,) = call(
        early_sums,
        (shape(users, depth, dtype=F32),),
        (adj, mine, other(mine), first, other(first)),
        flops=work // 2,
        nbytes=4 << 20,
    )
    own, *others = call(
        late_sums,
        (shape(share, depth, dtype=F32),) + (shape(share, depth),) * 3,
        (adj, early, second, other(second), middle, ends, other(middle), other(ends)),
        flops=work // 2,
        nbytes=4 << 20,
    )
    new_users, user_half = call(
        functools.partial(update, 4),
        (shape(share, depth, dtype=F32), shape(share, depth)),
        (own_emb, w_hi, w_lo, *(swap(others[k - 1], "ia", 4, k) for k in (3, 2, 1)), own),
        flops=12 * share * depth * depth,
        nbytes=3 << 20,
    )

    others_t = other(after(others_t, user_half))
    shares = [user_half] + [swap(user_half, "ia", 4, k) for k in (1, 2, 3)]
    shares += [other(x) for x in shares]
    (far,) = call(
        functools.partial(item_sums, (3,), 4),
        (shape(held, depth),),
        (adj_t, others_t, *shares),
        flops=work // 4,
        nbytes=2 << 20,
    )
    middle = send(far, back(MIDDLE))
    handed = send(far, back(HANDED))
    own, onward, near = call(
        functools.partial(item_sums, (0, 1, 2), 4),
        (shape(held, depth, dtype=F32), shape(held, depth, dtype=F32), shape(held, depth)),
        (adj_t, others_t, *shares, far),
        flops=3 * work // 4,
        nbytes=6 << 20,
    )
    near = send(near, back(TURN_2))
    (onward,) = call(pass_on, (shape(held, depth),), (onward, handed), nbytes=1 << 19)
    (new_items,) = call(
        functools.partial(update, 4, inner=1),
        (shape(held, depth, dtype=F32),),
        (item_emb, w_hi, w_lo, middle, own, near, send(onward, back(TURN_1))),
        flops=12 * held * depth * depth,
        nbytes=4 << 20,
    )
    return (new_users, new_items)


def gathered(n_au, n_ia, user_emb, item_emb, tiles, block_rows, block_cols, block_counts, w_self, w_inter):
    depth = w_self.shape[0]
    users, held = user_emb.shape[0], item_emb.shape[0]
    items = held * n_au
    share = users // n_ia
    work = 2 * users * items * depth

    blocks = lax.all_gather(item_emb.astype(BF16), "au", axis=0, tiled=True)
    (adj,) = call(
        functools.partial(dense, tiles.shape[2], False),
        (shape(users, items),),
        (block_rows, block_cols, block_counts, tiles),
        smem=3,
        nbytes=4 << 20,
    )
    (adj_t,) = call(functools.partial(flip, tiles.shape[2]), (shape(items, users),), (adj,), nbytes=4 << 20)
    w_hi, w_lo, own_emb = call(
        weights,
        (shape(2 * depth, depth), shape(2 * depth, depth), shape(share, depth, dtype=F32)),
        (user_emb, w_self, w_inter),
        nbytes=5 << 20,
    )
    (sums,) = call(
        user_sums, (shape(users, depth, dtype=F32),), (adj, blocks), flops=work, nbytes=6 << 20
    )
    sums = lax.psum_scatter(sums, "ia", scatter_dimension=0, tiled=True)
    new_users, user_half = call(
        functools.partial(update, 1),
        (shape(share, depth, dtype=F32), shape(share, depth)),
        (own_emb, w_hi, w_lo, sums),
        flops=12 * share * depth * depth,
        nbytes=3 << 20,
    )
    shares = lax.all_gather(user_half, "ia", axis=0, tiled=True)
    (sums,) = call(
        all_sums, (shape(items, depth, dtype=F32),), (adj_t, shares), flops=work, nbytes=6 << 20
    )
    sums = lax.psum_scatter(sums, "au", scatter_dimension=0, tiled=True)
    (new_items,) = call(
        functools.partial(update, 1),
        (shape(held, depth, dtype=F32),),
        (item_emb, w_hi, w_lo, sums),
        flops=12 * held * depth * depth,
        nbytes=4 << 20,
    )
    return (new_users, new_items)


def local(n_au, n_ia, user_emb, item_emb, tiles, *rest):
    edge = tiles.shape[2]
    if (n_au, n_ia) == (8, 4) and item_emb.shape[0] == edge and edge % (user_emb.shape[0] // n_ia) == 0:
        return in_turns(user_emb, item_emb, tiles, *rest)
    return gathered(n_au, n_ia, user_emb, item_emb, tiles, *rest)


def solution(mesh):
    in_specs = (
        P("au", None),
        P(("ia", "au"), None),
        P("au", "ia", None, None),
        P("au", "ia"),
        P("au", "ia"),
        P("au", "ia"),
        P(),
        P(),
    )
    out_specs = (P(("au", "ia"), None), P(("ia", "au"), None))
    return jax.shard_map(
        functools.partial(local, mesh.shape["au"], mesh.shape["ia"]),
        mesh=mesh,
        in_specs=in_specs,
        out_specs=out_specs,
        check_vma=False,
    )
```

```python
import functools

import jax
import jax.numpy as jnp
from jax import lax
from jax.experimental import pallas as pl
from jax.experimental.pallas import tpu as pltpu
from jax.sharding import PartitionSpec as P

F32 = jnp.float32
BF16 = jnp.bfloat16
VMEM = pl.BlockSpec(memory_space=pltpu.VMEM)
SMEM = pl.BlockSpec(memory_space=pltpu.SMEM)
PARAMS = pltpu.CompilerParams(vmem_limit_bytes=40 * 1024 * 1024)

TURN_1 = ((0, 2), (3, 1), (1, 0), (2, 3))
TURN_2 = ((0, 1), (3, 2), (1, 3), (2, 0))
MIDDLE = ((1, 2), (2, 1), (0, 0), (3, 3))
HANDED = ((2, 3), (1, 0), (3, 2), (0, 1))
FAR = ((0, 3), (3, 0), (1, 2), (2, 1))


def back(pairs):
    return tuple((b, a) for a, b in pairs)


def send(x, pairs):
    return lax.ppermute(x, "au", [(2 * a + core, 2 * b + core) for a, b in pairs for core in (0, 1)])


def swap(x, axis, n, by):
    return lax.ppermute(x, axis, [(i, i ^ by) for i in range(n)])


def slot_of(me, block):
    apart = block ^ me
    turn = apart >> 1
    swapped = in_middle() & ((turn == 1) | (turn == 2))
    return jnp.where(swapped, 3 - turn, turn) * 2 + (apart & 1)


def in_middle():
    z = lax.axis_index("au") >> 1
    return (z == 1) | (z == 2)


def call(kernel, out_shape, operands, smem=0, flops=0, nbytes=0):
    return pl.pallas_call(
        kernel,
        out_shape=out_shape,
        in_specs=[SMEM] * smem + [VMEM] * (len(operands) - smem),
        out_specs=jax.tree.map(lambda _: VMEM, out_shape),
        compiler_params=PARAMS,
        cost_estimate=pl.CostEstimate(flops=flops, bytes_accessed=nbytes, transcendentals=0),
    )(*operands)


def shape(*dims, dtype=BF16):
    return jax.ShapeDtypeStruct(dims, dtype)


def split(x):
    hi = x.astype(BF16)
    return hi, (x - hi.astype(F32)).astype(BF16)


def dot(a, b):
    return jnp.dot(a, b, preferred_element_type=F32)


def total(refs):
    value = refs[0][...].astype(F32)
    for ref in refs[1:]:
        value = value + ref[...].astype(F32)
    return value


def dense(piece, turns, rows, cols, count, tiles, adj):
    edge = tiles.shape[2]
    adj[...] = jnp.zeros_like(adj)

    def place(slot, carry):
        at = cols[0, slot]
        if turns:
            at = slot_of(lax.axis_index("au"), at)
        col = pl.multiple_of(at * edge, edge)
        for part in range(edge // piece):
            row = rows[0, slot] * (edge // piece) + part
            if turns:
                row = row ^ lax.axis_index("ia")
            row = pl.multiple_of(row * piece, piece)
            adj[pl.ds(row, piece), pl.ds(col, edge)] = tiles[0, slot, part * piece : (part + 1) * piece, :]
        return carry

    lax.fori_loop(0, count[0, 0], place, 0)


def flip(edge, adj, *outs):
    n = len(outs)
    for k in range(adj.shape[1] // edge):
        out = outs[k % n]
        out[k // n * edge : (k // n + 1) * edge, :] = adj[:, k * edge : (k + 1) * edge].T


def ready(edge, adj, user_emb, w_self, w_inter, w_hi, w_lo, own, *adj_t):
    weights(user_emb, w_self, w_inter, w_hi, w_lo, own)
    flip(edge, adj, *adj_t)


def weights(user_emb, w_self, w_inter, w_hi, w_lo, own):
    depth = w_self.shape[0]
    for k, w in enumerate((w_self, w_inter)):
        w_hi[k * depth : (k + 1) * depth, :], w_lo[k * depth : (k + 1) * depth, :] = split(w[...])
    height = own.shape[0]
    own[...] = user_emb[pl.ds(pl.multiple_of(lax.axis_index("ia") * height, height), height), :]


def block_sums(adj, first, blocks):
    edge = blocks[0].shape[0]
    return sum(dot(adj[:, (first + k) * edge : (first + k + 1) * edge], block) for k, block in enumerate(blocks))


def early_sums(adj, *refs):
    *blocks, sums = refs
    sums[...] = block_sums(adj, 0, [block[...] for block in blocks])


def late_sums(adj, early, middle, ends, middle_other, ends_other, *outs):
    inner = in_middle()
    blocks = [jnp.where(inner, a[...], b[...]) for a, b in ((middle, ends), (middle_other, ends_other))]
    sums = early[...] + block_sums(adj, 6, blocks)
    height = outs[0].shape[0]
    for k, out in enumerate(outs):
        out[...] = sums[k * height : (k + 1) * height].astype(out.dtype)


def user_sums(adj, items, out):
    out[...] = dot(adj[...], items[...])


def item_sums(starts, n, *refs):
    adj_t, shares, outs = refs[:2], refs[2 : 2 + 2 * n], refs[-len(starts) :]
    users = [jnp.concatenate([share[...] for share in shares[core * n : core * n + n]], axis=0) for core in (0, 1)]
    for start, out in zip(starts, outs):
        rows = slice(start, start + out.shape[0])
        out[...] = (dot(adj_t[0][rows, :], users[0]) + dot(adj_t[1][rows, :], users[1])).astype(out.dtype)


def all_sums(adj_t, users, out):
    out[...] = dot(adj_t[...], users[...])


def pass_on(sums, handed, out):
    direct = out.shape[0] - handed.shape[0]
    out[:direct, :] = sums[:direct, :].astype(out.dtype)
    out[direct:, :] = (sums[direct:, :] + jnp.where(in_middle(), handed[...].astype(F32), 0)).astype(out.dtype)


def mix(side, own, w_hi, w_lo):
    height = own.shape[0]
    hi, lo = split(jnp.concatenate([side + own, side * own], axis=1))
    both = dot(jnp.concatenate([hi, lo], axis=0), w_hi)
    mixed = both[:height] + (both[height:] + dot(hi, w_lo))
    return jnp.where(mixed >= 0, mixed, 0.2 * mixed)


def update(n, emb, w_hi, w_lo, *refs):
    mixed = mix(total(refs[:n]), emb[...], w_hi[...], w_lo[...])
    for out in refs[n:]:
        out[...] = mixed.astype(out.dtype)


def last_update(emb, w_hi, w_lo, own, near, onward, far, middle, new_users, out, new_users_out, sem):
    copy = pltpu.make_async_copy(new_users, new_users_out, sem)
    copy.start()
    side = total((own, near, onward))
    rest = jnp.where(in_middle(), middle[...].astype(F32), 0)
    side = side + jnp.concatenate([far[...].astype(F32), rest], axis=0)
    out[...] = mix(side, emb[...], w_hi[...], w_lo[...])
    copy.wait()


def in_turns(user_emb, item_emb, tiles, block_rows, block_cols, block_counts, w_self, w_inter):
    depth = w_self.shape[0]
    users, held = user_emb.shape[0], item_emb.shape[0]
    items = held * 8
    share = users // 4
    work = 2 * users * items * depth

    def other(x):
        return swap(x, "au", 8, 1)

    def after(x, *done):
        return lax.optimization_barrier((x, *done))[0]

    mine = item_emb.astype(BF16)
    first = send(mine, TURN_1)
    (adj,) = call(
        functools.partial(dense, share, True),
        (shape(users, items),),
        (block_rows, block_cols, block_counts, tiles),
        smem=3,
        nbytes=8 << 20,
    )
    second = send(after(mine, adj), TURN_2)
    w_hi, w_lo, own_emb, adj_t, others_t = call(
        functools.partial(ready, held),
        (shape(2 * depth, depth), shape(2 * depth, depth), shape(share, depth, dtype=F32))
        + (shape(items // 2, users), shape(items // 2, users)),
        (adj, user_emb, w_self, w_inter),
        nbytes=9 << 20,
    )
    middle = send(after(mine, w_hi), MIDDLE)
    first = after(first, w_hi)
    ends = send(first, HANDED)
    (early,) = call(
        early_sums,
        (shape(users, depth, dtype=F32),),
        (adj, mine, other(mine), first, other(first), second, other(second)),
        flops=work // 2,
        nbytes=4 << 20,
    )
    own, *others = call(
        late_sums,
        (shape(share, depth, dtype=F32),) + (shape(share, depth),) * 3,
        (adj, early, middle, ends, other(middle), other(ends)),
        flops=work // 2,
        nbytes=4 << 20,
    )
    others_t = other(after(others_t, own))
    own = after(own, others_t)
    new_users, user_half = call(
        functools.partial(update, 4),
        (shape(share, depth, dtype=F32), shape(share, depth)),
        (own_emb, w_hi, w_lo, *(swap(others[k - 1], "ia", 4, k) for k in (3, 2, 1)), own),
        flops=12 * share * depth * depth,
        nbytes=3 << 20,
    )

    shares = [user_half] + [swap(user_half, "ia", 4, k) for k in (1, 2, 3)]
    shares += [other(x) for x in shares]
    direct = 160
    far, handed = call(
        functools.partial(item_sums, (3 * held, 3 * held + direct), 4),
        (shape(direct, depth), shape(held - direct, depth)),
        (adj_t, others_t, *shares),
        flops=work // 4,
        nbytes=2 << 20,
    )
    middle_in = handed
    handed = send(handed, back(HANDED))
    far = send(far, FAR)
    own, onward, near = call(
        functools.partial(item_sums, (0, held, 2 * held), 4),
        (shape(held, depth, dtype=F32), shape(held, depth, dtype=F32), shape(held, depth)),
        (adj_t, others_t, *shares),
        flops=3 * work // 4,
        nbytes=6 << 20,
    )
    middle = send(middle_in, back(MIDDLE))
    near = send(near, back(TURN_2))
    (onward,) = call(pass_on, (shape(held, depth),), (after(onward, far), handed), nbytes=1 << 19)
    new_items, new_users = pl.pallas_call(
        last_update,
        out_shape=(shape(held, depth, dtype=F32), shape(share, depth, dtype=F32)),
        in_specs=[VMEM] * 9,
        out_specs=(VMEM, pl.BlockSpec(memory_space=pl.ANY)),
        scratch_shapes=(pltpu.SemaphoreType.DMA,),
        compiler_params=PARAMS,
        cost_estimate=pl.CostEstimate(flops=12 * held * depth * depth, bytes_accessed=4 << 20, transcendentals=0),
    )(item_emb, w_hi, w_lo, own, near, send(onward, back(TURN_1)), far, middle, new_users)
    return (new_users, new_items)


def gathered(n_au, n_ia, user_emb, item_emb, tiles, block_rows, block_cols, block_counts, w_self, w_inter):
    depth = w_self.shape[0]
    users, held = user_emb.shape[0], item_emb.shape[0]
    items = held * n_au
    share = users // n_ia
    work = 2 * users * items * depth

    blocks = lax.all_gather(item_emb.astype(BF16), "au", axis=0, tiled=True)
    (adj,) = call(
        functools.partial(dense, tiles.shape[2], False),
        (shape(users, items),),
        (block_rows, block_cols, block_counts, tiles),
        smem=3,
        nbytes=4 << 20,
    )
    (adj_t,) = call(functools.partial(flip, tiles.shape[2]), (shape(items, users),), (adj,), nbytes=4 << 20)
    w_hi, w_lo, own_emb = call(
        weights,
        (shape(2 * depth, depth), shape(2 * depth, depth), shape(share, depth, dtype=F32)),
        (user_emb, w_self, w_inter),
        nbytes=5 << 20,
    )
    (sums,) = call(
        user_sums, (shape(users, depth, dtype=F32),), (adj, blocks), flops=work, nbytes=6 << 20
    )
    sums = lax.psum_scatter(sums, "ia", scatter_dimension=0, tiled=True)
    new_users, user_half = call(
        functools.partial(update, 1),
        (shape(share, depth, dtype=F32), shape(share, depth)),
        (own_emb, w_hi, w_lo, sums),
        flops=12 * share * depth * depth,
        nbytes=3 << 20,
    )
    shares = lax.all_gather(user_half, "ia", axis=0, tiled=True)
    (sums,) = call(
        all_sums, (shape(items, depth, dtype=F32),), (adj_t, shares), flops=work, nbytes=6 << 20
    )
    sums = lax.psum_scatter(sums, "au", scatter_dimension=0, tiled=True)
    (new_items,) = call(
        functools.partial(update, 1),
        (shape(held, depth, dtype=F32),),
        (item_emb, w_hi, w_lo, sums),
        flops=12 * held * depth * depth,
        nbytes=4 << 20,
    )
    return (new_users, new_items)


def local(n_au, n_ia, user_emb, item_emb, tiles, *rest):
    edge = tiles.shape[2]
    if (n_au, n_ia) == (8, 4) and item_emb.shape[0] == edge and edge % (user_emb.shape[0] // n_ia) == 0:
        return in_turns(user_emb, item_emb, tiles, *rest)
    return gathered(n_au, n_ia, user_emb, item_emb, tiles, *rest)


def solution(mesh):
    in_specs = (
        P("au", None),
        P(("ia", "au"), None),
        P("au", "ia", None, None),
        P("au", "ia"),
        P("au", "ia"),
        P("au", "ia"),
        P(),
        P(),
    )
    out_specs = (P(("au", "ia"), None), P(("ia", "au"), None))
    return jax.shard_map(
        functools.partial(local, mesh.shape["au"], mesh.shape["ia"]),
        mesh=mesh,
        in_specs=in_specs,
        out_specs=out_specs,
        check_vma=False,
    )
```

```python
import functools

import jax
import jax.numpy as jnp
from jax import lax
from jax.experimental import pallas as pl
from jax.experimental.pallas import tpu as pltpu
from jax.sharding import PartitionSpec as P

F32 = jnp.float32
BF16 = jnp.bfloat16
VMEM = pl.BlockSpec(memory_space=pltpu.VMEM)
SMEM = pl.BlockSpec(memory_space=pltpu.SMEM)
PARAMS = pltpu.CompilerParams(vmem_limit_bytes=40 * 1024 * 1024)

TURN_1 = ((0, 2), (3, 1), (1, 0), (2, 3))
TURN_2 = ((0, 1), (3, 2), (1, 3), (2, 0))
MIDDLE = ((1, 2), (2, 1))
HANDED = ((2, 3), (1, 0), (3, 2), (0, 1))


def back(pairs):
    return tuple((b, a) for a, b in pairs)


def send(x, pairs):
    perm = [(2 * a + core, 2 * b + core) for a, b in pairs for core in (0, 1)]
    perm += [(i, i ^ 1) for i in range(8) if i // 2 not in [a for a, _ in pairs]]
    return lax.ppermute(x, "au", perm)


def swap(x, axis, n, by):
    return lax.ppermute(x, axis, [(i, i ^ by) for i in range(n)])


def slot_of(me, block):
    apart = block ^ me
    turn = apart >> 1
    swapped = in_middle() & ((turn == 1) | (turn == 2))
    return jnp.where(swapped, 3 - turn, turn) * 2 + (apart & 1)


def in_middle():
    z = lax.axis_index("au") >> 1
    return (z == 1) | (z == 2)


def call(kernel, out_shape, operands, smem=0, flops=0, nbytes=0):
    return pl.pallas_call(
        kernel,
        out_shape=out_shape,
        in_specs=[SMEM] * smem + [VMEM] * (len(operands) - smem),
        out_specs=jax.tree.map(lambda _: VMEM, out_shape),
        compiler_params=PARAMS,
        cost_estimate=pl.CostEstimate(flops=flops, bytes_accessed=nbytes, transcendentals=0),
    )(*operands)


def shape(*dims, dtype=BF16):
    return jax.ShapeDtypeStruct(dims, dtype)


def split(x):
    hi = x.astype(BF16)
    return hi, (x - hi.astype(F32)).astype(BF16)


def dot(a, b):
    return jnp.dot(a, b, preferred_element_type=F32)


def total(refs):
    value = refs[0][...].astype(F32)
    for ref in refs[1:]:
        value = value + ref[...].astype(F32)
    return value


def dense(piece, turns, rows, cols, count, tiles, adj):
    edge = tiles.shape[2]
    adj[...] = jnp.zeros_like(adj)

    def place(slot, carry):
        at = cols[0, slot]
        if turns:
            at = slot_of(lax.axis_index("au"), at)
        col = pl.multiple_of(at * edge, edge)
        for part in range(edge // piece):
            row = rows[0, slot] * (edge // piece) + part
            if turns:
                row = row ^ lax.axis_index("ia")
            row = pl.multiple_of(row * piece, piece)
            adj[pl.ds(row, piece), pl.ds(col, edge)] = tiles[0, slot, part * piece : (part + 1) * piece, :]
        return carry

    lax.fori_loop(0, count[0, 0], place, 0)


def flip(edge, adj, *outs):
    n = len(outs)
    for k in range(adj.shape[1] // edge):
        out = outs[k % n]
        out[k // n * edge : (k // n + 1) * edge, :] = adj[:, k * edge : (k + 1) * edge].T


def ready(edge, adj, user_emb, w_self, w_inter, w_hi, w_lo, own, *adj_t):
    weights(user_emb, w_self, w_inter, w_hi, w_lo, own)
    flip(edge, adj, *adj_t)


def weights(user_emb, w_self, w_inter, w_hi, w_lo, own):
    depth = w_self.shape[0]
    for k, w in enumerate((w_self, w_inter)):
        w_hi[k * depth : (k + 1) * depth, :], w_lo[k * depth : (k + 1) * depth, :] = split(w[...])
    height = own.shape[0]
    own[...] = user_emb[pl.ds(pl.multiple_of(lax.axis_index("ia") * height, height), height), :]


def block_sums(adj, first, blocks):
    edge = blocks[0].shape[0]
    return sum(dot(adj[:, (first + k) * edge : (first + k + 1) * edge], block) for k, block in enumerate(blocks))


def early_sums(adj, *refs):
    *blocks, sums = refs
    sums[...] = block_sums(adj, 0, [block[...] for block in blocks])


def late_sums(adj, early, middle, ends, middle_other, ends_other, *outs):
    inner = in_middle()
    blocks = [jnp.where(inner, a[...], b[...]) for a, b in ((middle, ends), (middle_other, ends_other))]
    sums = early[...] + block_sums(adj, 6, blocks)
    height = outs[0].shape[0]
    for k, out in enumerate(outs):
        out[...] = sums[k * height : (k + 1) * height].astype(out.dtype)


def user_sums(adj, items, out):
    out[...] = dot(adj[...], items[...])


def item_sums(slots, n, *refs):
    adj_t, shares, outs = refs[:2], refs[2 : 2 + 2 * n], refs[-len(slots) :]
    users = [jnp.concatenate([share[...] for share in shares[core * n : core * n + n]], axis=0) for core in (0, 1)]
    edge = outs[0].shape[0]
    for slot, out in zip(slots, outs):
        rows = slice(slot * edge, (slot + 1) * edge)
        out[...] = (dot(adj_t[0][rows, :], users[0]) + dot(adj_t[1][rows, :], users[1])).astype(out.dtype)


def item_sums_and(starts, n, *refs):
    refs[-1][...] = refs[-len(starts) - 2][...]
    item_sums(starts, n, *refs[: -len(starts) - 2], *refs[-len(starts) - 1 : -1])


def all_sums(adj_t, users, out):
    out[...] = dot(adj_t[...], users[...])


def pass_on(sums, handed, out):
    given = jnp.where(in_middle(), handed[...].astype(F32), 0)
    out[...] = (sums[...] + given).astype(out.dtype)


def mix(side, own, w_hi, w_lo):
    height = own.shape[0]
    hi, lo = split(jnp.concatenate([side + own, side * own], axis=1))
    both = dot(jnp.concatenate([hi, lo], axis=0), w_hi)
    mixed = both[:height] + (both[height:] + dot(hi, w_lo))
    return jnp.where(mixed >= 0, mixed, 0.2 * mixed)


def update(n, emb, w_hi, w_lo, *refs):
    mixed = mix(total(refs[:n]), emb[...], w_hi[...], w_lo[...])
    for out in refs[n:]:
        out[...] = mixed.astype(out.dtype)


def last_update(emb, w_hi, w_lo, middle, own, near, onward, out, ready, sems):
    inner = in_middle()
    n = sems.shape[0]
    copies = []
    for k in range(n):
        rows = slice(k * (out.shape[0] // n), (k + 1) * (out.shape[0] // n))
        side = own[rows, :] + near[rows, :].astype(F32) + onward[rows, :].astype(F32)
        side = side + jnp.where(inner, middle[rows, :].astype(F32), 0)
        ready[rows, :] = mix(side, emb[rows, :], w_hi[...], w_lo[...])
        copies.append(pltpu.make_async_copy(ready.at[rows, :], out.at[rows, :], sems.at[k]))
        copies[k].start()
    for copy in copies:
        copy.wait()


def in_turns(user_emb, item_emb, tiles, block_rows, block_cols, block_counts, w_self, w_inter):
    depth = w_self.shape[0]
    users, held = user_emb.shape[0], item_emb.shape[0]
    items = held * 8
    share = users // 4
    work = 2 * users * items * depth

    def other(x):
        return swap(x, "au", 8, 1)

    def after(x, *done):
        return lax.optimization_barrier((x, *done))[0]

    mine = item_emb.astype(BF16)
    first = send(mine, TURN_1)
    (adj,) = call(
        functools.partial(dense, share, True),
        (shape(users, items),),
        (block_rows, block_cols, block_counts, tiles),
        smem=3,
        nbytes=8 << 20,
    )
    second = send(after(mine, adj), TURN_2)
    w_hi, w_lo, own_emb, adj_t, others_t = call(
        functools.partial(ready, held),
        (shape(2 * depth, depth), shape(2 * depth, depth), shape(share, depth, dtype=F32))
        + (shape(items // 2, users), shape(items // 2, users)),
        (adj, user_emb, w_self, w_inter),
        nbytes=9 << 20,
    )
    middle = send(after(mine, w_hi), MIDDLE)
    first = after(first, w_hi)
    ends = send(first, HANDED)
    (early,) = call(
        early_sums,
        (shape(users, depth, dtype=F32),),
        (adj, mine, other(mine), first, other(first), second, other(second)),
        flops=work // 2,
        nbytes=4 << 20,
    )
    own, *others = call(
        late_sums,
        (shape(share, depth, dtype=F32),) + (shape(share, depth),) * 3,
        (adj, early, middle, ends, other(middle), other(ends)),
        flops=work // 2,
        nbytes=4 << 20,
    )
    others_t = other(after(others_t, own))
    own = after(own, others_t)
    new_users, user_half = call(
        functools.partial(update, 4),
        (shape(share, depth, dtype=F32), shape(share, depth)),
        (own_emb, w_hi, w_lo, *(swap(others[k - 1], "ia", 4, k) for k in (3, 2, 1)), own),
        flops=12 * share * depth * depth,
        nbytes=3 << 20,
    )

    shares = [user_half] + [swap(user_half, "ia", 4, k) for k in (1, 2, 3)]
    shares += [other(x) for x in shares]
    (far,) = call(
        functools.partial(item_sums, (3,), 4),
        (shape(held, depth),),
        (adj_t, others_t, *shares),
        flops=work // 4,
        nbytes=2 << 20,
    )
    middle = send(far, back(MIDDLE))
    handed = send(far, back(HANDED))
    own, onward = call(
        functools.partial(item_sums, (0, 1), 4),
        (shape(held, depth, dtype=F32), shape(held, depth, dtype=F32)),
        (adj_t, others_t, *shares, far),
        flops=3 * work // 4,
        nbytes=6 << 20,
    )
    near, new_users = call(
        functools.partial(item_sums_and, (2,), 4),
        (shape(held, depth), shape(share, depth, dtype=F32)),
        (adj_t, others_t, *shares, own, new_users),
        flops=work // 4,
        nbytes=2 << 20,
    )
    near = send(near, back(TURN_2))
    (onward,) = call(pass_on, (shape(held, depth),), (onward, handed), nbytes=1 << 19)
    new_items = pl.pallas_call(
        last_update,
        out_shape=shape(held, depth, dtype=F32),
        in_specs=[VMEM] * 7,
        out_specs=pl.BlockSpec(memory_space=pl.ANY),
        scratch_shapes=(pltpu.VMEM((held, depth), F32), pltpu.SemaphoreType.DMA((2,))),
        compiler_params=PARAMS,
        cost_estimate=pl.CostEstimate(flops=12 * held * depth * depth, bytes_accessed=4 << 20, transcendentals=0),
    )(item_emb, w_hi, w_lo, middle, own, near, send(onward, back(TURN_1)))
    return (new_users, new_items)


def gathered(n_au, n_ia, user_emb, item_emb, tiles, block_rows, block_cols, block_counts, w_self, w_inter):
    depth = w_self.shape[0]
    users, held = user_emb.shape[0], item_emb.shape[0]
    items = held * n_au
    share = users // n_ia
    work = 2 * users * items * depth

    blocks = lax.all_gather(item_emb.astype(BF16), "au", axis=0, tiled=True)
    (adj,) = call(
        functools.partial(dense, tiles.shape[2], False),
        (shape(users, items),),
        (block_rows, block_cols, block_counts, tiles),
        smem=3,
        nbytes=4 << 20,
    )
    (adj_t,) = call(functools.partial(flip, tiles.shape[2]), (shape(items, users),), (adj,), nbytes=4 << 20)
    w_hi, w_lo, own_emb = call(
        weights,
        (shape(2 * depth, depth), shape(2 * depth, depth), shape(share, depth, dtype=F32)),
        (user_emb, w_self, w_inter),
        nbytes=5 << 20,
    )
    (sums,) = call(
        user_sums, (shape(users, depth, dtype=F32),), (adj, blocks), flops=work, nbytes=6 << 20
    )
    sums = lax.psum_scatter(sums, "ia", scatter_dimension=0, tiled=True)
    new_users, user_half = call(
        functools.partial(update, 1),
        (shape(share, depth, dtype=F32), shape(share, depth)),
        (own_emb, w_hi, w_lo, sums),
        flops=12 * share * depth * depth,
        nbytes=3 << 20,
    )
    shares = lax.all_gather(user_half, "ia", axis=0, tiled=True)
    (sums,) = call(
        all_sums, (shape(items, depth, dtype=F32),), (adj_t, shares), flops=work, nbytes=6 << 20
    )
    sums = lax.psum_scatter(sums, "au", scatter_dimension=0, tiled=True)
    (new_items,) = call(
        functools.partial(update, 1),
        (shape(held, depth, dtype=F32),),
        (item_emb, w_hi, w_lo, sums),
        flops=12 * held * depth * depth,
        nbytes=4 << 20,
    )
    return (new_users, new_items)


def local(n_au, n_ia, user_emb, item_emb, tiles, *rest):
    edge = tiles.shape[2]
    if (n_au, n_ia) == (8, 4) and item_emb.shape[0] == edge and edge % (user_emb.shape[0] // n_ia) == 0:
        return in_turns(user_emb, item_emb, tiles, *rest)
    return gathered(n_au, n_ia, user_emb, item_emb, tiles, *rest)


def solution(mesh):
    in_specs = (
        P("au", None),
        P(("ia", "au"), None),
        P("au", "ia", None, None),
        P("au", "ia"),
        P("au", "ia"),
        P("au", "ia"),
        P(),
        P(),
    )
    out_specs = (P(("au", "ia"), None), P(("ia", "au"), None))
    return jax.shard_map(
        functools.partial(local, mesh.shape["au"], mesh.shape["ia"]),
        mesh=mesh,
        in_specs=in_specs,
        out_specs=out_specs,
        check_vma=False,
    )
```

```python
import functools

import jax
import jax.numpy as jnp
from jax import lax
from jax.experimental import pallas as pl
from jax.experimental.pallas import tpu as pltpu
from jax.sharding import PartitionSpec as P

F32 = jnp.float32
BF16 = jnp.bfloat16
VMEM = pl.BlockSpec(memory_space=pltpu.VMEM)
SMEM = pl.BlockSpec(memory_space=pltpu.SMEM)
PARAMS = pltpu.CompilerParams(vmem_limit_bytes=40 * 1024 * 1024)

TURN_1 = ((0, 2), (3, 1), (1, 0), (2, 3))
TURN_2 = ((0, 1), (3, 2), (1, 3), (2, 0))
MIDDLE = ((1, 2), (2, 1))
HANDED = ((2, 3), (1, 0), (3, 2), (0, 1))


def back(pairs):
    return tuple((b, a) for a, b in pairs)


def send(x, pairs):
    perm = [(2 * a + core, 2 * b + core) for a, b in pairs for core in (0, 1)]
    perm += [(i, i ^ 1) for i in range(8) if i // 2 not in [a for a, _ in pairs]]
    return lax.ppermute(x, "au", perm)


def swap(x, axis, n, by):
    return lax.ppermute(x, axis, [(i, i ^ by) for i in range(n)])


def slot_of(me, block):
    apart = block ^ me
    turn = apart >> 1
    swapped = in_middle() & ((turn == 1) | (turn == 2))
    return jnp.where(swapped, 3 - turn, turn) * 2 + (apart & 1)


def in_middle():
    z = lax.axis_index("au") >> 1
    return (z == 1) | (z == 2)


def call(kernel, out_shape, operands, smem=0, flops=0, nbytes=0):
    return pl.pallas_call(
        kernel,
        out_shape=out_shape,
        in_specs=[SMEM] * smem + [VMEM] * (len(operands) - smem),
        out_specs=jax.tree.map(lambda _: VMEM, out_shape),
        compiler_params=PARAMS,
        cost_estimate=pl.CostEstimate(flops=flops, bytes_accessed=nbytes, transcendentals=0),
    )(*operands)


def shape(*dims, dtype=BF16):
    return jax.ShapeDtypeStruct(dims, dtype)


def split(x):
    hi = x.astype(BF16)
    return hi, (x - hi.astype(F32)).astype(BF16)


def dot(a, b):
    return jnp.dot(a, b, preferred_element_type=F32)


def total(refs):
    value = refs[0][...].astype(F32)
    for ref in refs[1:]:
        value = value + ref[...].astype(F32)
    return value


def dense(piece, turns, rows, cols, count, tiles, adj):
    edge = tiles.shape[2]
    adj[...] = jnp.zeros_like(adj)

    def place(slot, carry):
        at = cols[0, slot]
        if turns:
            at = slot_of(lax.axis_index("au"), at)
        col = pl.multiple_of(at * edge, edge)
        for part in range(edge // piece):
            row = rows[0, slot] * (edge // piece) + part
            if turns:
                row = row ^ lax.axis_index("ia")
            row = pl.multiple_of(row * piece, piece)
            adj[pl.ds(row, piece), pl.ds(col, edge)] = tiles[0, slot, part * piece : (part + 1) * piece, :]
        return carry

    lax.fori_loop(0, count[0, 0], place, 0)


def flip(edge, adj, *outs):
    n = len(outs)
    for k in range(adj.shape[1] // edge):
        out = outs[k % n]
        out[k // n * edge : (k // n + 1) * edge, :] = adj[:, k * edge : (k + 1) * edge].T


def ready(edge, adj, user_emb, w_self, w_inter, w_hi, w_lo, own, *adj_t):
    weights(user_emb, w_self, w_inter, w_hi, w_lo, own)
    flip(edge, adj, *adj_t)


def weights(user_emb, w_self, w_inter, w_hi, w_lo, own):
    depth = w_self.shape[0]
    for k, w in enumerate((w_self, w_inter)):
        w_hi[k * depth : (k + 1) * depth, :], w_lo[k * depth : (k + 1) * depth, :] = split(w[...])
    height = own.shape[0]
    own[...] = user_emb[pl.ds(pl.multiple_of(lax.axis_index("ia") * height, height), height), :]


def block_sums(adj, first, blocks):
    edge = blocks[0].shape[0]
    return sum(dot(adj[:, (first + k) * edge : (first + k + 1) * edge], block) for k, block in enumerate(blocks))


def early_sums(adj, *refs):
    *blocks, middle, ends, sums = refs
    blocks = [block[...] for block in blocks] + [jnp.where(in_middle(), middle[...], ends[...])]
    sums[...] = block_sums(adj, 0, blocks)


def late_sums(adj, early, middle, ends, *outs):
    sums = early[...] + block_sums(adj, 7, [jnp.where(in_middle(), middle[...], ends[...])])
    height = outs[0].shape[0]
    for k, out in enumerate(outs):
        out[...] = sums[k * height : (k + 1) * height].astype(out.dtype)


def user_sums(adj, items, out):
    out[...] = dot(adj[...], items[...])


def item_sums(slots, n, *refs):
    adj_t, shares, outs = refs[:2], refs[2 : 2 + 2 * n], refs[-len(slots) :]
    users = [jnp.concatenate([share[...] for share in shares[core * n : core * n + n]], axis=0) for core in (0, 1)]
    edge = outs[0].shape[0]
    for slot, out in zip(slots, outs):
        rows = slice(slot * edge, (slot + 1) * edge)
        out[...] = (dot(adj_t[0][rows, :], users[0]) + dot(adj_t[1][rows, :], users[1])).astype(out.dtype)


def item_sums_and(starts, n, *refs):
    refs[-1][...] = refs[-len(starts) - 2][...]
    item_sums(starts, n, *refs[: -len(starts) - 2], *refs[-len(starts) - 1 : -1])


def all_sums(adj_t, users, out):
    out[...] = dot(adj_t[...], users[...])


def pass_on(sums, handed, out):
    given = jnp.where(in_middle(), handed[...].astype(F32), 0)
    out[...] = (sums[...] + given).astype(out.dtype)


def mix(side, own, w_hi, w_lo):
    height = own.shape[0]
    hi, lo = split(jnp.concatenate([side + own, side * own], axis=1))
    both = dot(jnp.concatenate([hi, lo], axis=0), w_hi)
    mixed = both[:height] + (both[height:] + dot(hi, w_lo))
    return jnp.where(mixed >= 0, mixed, 0.2 * mixed)


def update(n, emb, w_hi, w_lo, *refs):
    mixed = mix(total(refs[:n]), emb[...], w_hi[...], w_lo[...])
    for out in refs[n:]:
        out[...] = mixed.astype(out.dtype)


def last_update(emb, w_hi, w_lo, middle, own, near, onward, out, ready, sems):
    inner = in_middle()
    n = sems.shape[0]
    copies = []
    for k in range(n):
        rows = slice(k * (out.shape[0] // n), (k + 1) * (out.shape[0] // n))
        side = own[rows, :] + near[rows, :].astype(F32) + onward[rows, :].astype(F32)
        side = side + jnp.where(inner, middle[rows, :].astype(F32), 0)
        ready[rows, :] = mix(side, emb[rows, :], w_hi[...], w_lo[...])
        copies.append(pltpu.make_async_copy(ready.at[rows, :], out.at[rows, :], sems.at[k]))
        copies[k].start()
    for copy in copies:
        copy.wait()


def in_turns(user_emb, item_emb, tiles, block_rows, block_cols, block_counts, w_self, w_inter):
    depth = w_self.shape[0]
    users, held = user_emb.shape[0], item_emb.shape[0]
    items = held * 8
    share = users // 4
    work = 2 * users * items * depth

    def other(x):
        return swap(x, "au", 8, 1)

    def after(x, *done):
        return lax.optimization_barrier((x, *done))[0]

    mine = item_emb.astype(BF16)
    first = send(mine, TURN_1)
    (adj,) = call(
        functools.partial(dense, share, True),
        (shape(users, items),),
        (block_rows, block_cols, block_counts, tiles),
        smem=3,
        nbytes=8 << 20,
    )
    second = send(after(mine, adj), TURN_2)
    w_hi, w_lo, own_emb, adj_t, others_t = call(
        functools.partial(ready, held),
        (shape(2 * depth, depth), shape(2 * depth, depth), shape(share, depth, dtype=F32))
        + (shape(items // 2, users), shape(items // 2, users)),
        (adj, user_emb, w_self, w_inter),
        nbytes=9 << 20,
    )
    middle = send(after(mine, w_hi), MIDDLE)
    first = after(first, w_hi)
    ends = send(first, HANDED)
    (early,) = call(
        early_sums,
        (shape(users, depth, dtype=F32),),
        (adj, mine, other(mine), first, other(first), second, other(second), middle, ends),
        flops=work // 2,
        nbytes=4 << 20,
    )
    own, *others = call(
        late_sums,
        (shape(share, depth, dtype=F32),) + (shape(share, depth),) * 3,
        (adj, early, other(middle), other(ends)),
        flops=work // 2,
        nbytes=4 << 20,
    )
    others_t = other(after(others_t, own))
    own = after(own, others_t)
    new_users, user_half = call(
        functools.partial(update, 4),
        (shape(share, depth, dtype=F32), shape(share, depth)),
        (own_emb, w_hi, w_lo, *(swap(others[k - 1], "ia", 4, k) for k in (1, 2, 3)), own),
        flops=12 * share * depth * depth,
        nbytes=3 << 20,
    )

    shares = [user_half] + [swap(user_half, "ia", 4, k) for k in (1, 2, 3)]
    shares[1:3] = lax.optimization_barrier(tuple(shares[1:3]))
    shares += [other(x) for x in shares]
    (far,) = call(
        functools.partial(item_sums, (3,), 4),
        (shape(held, depth),),
        (adj_t, others_t, *shares),
        flops=work // 4,
        nbytes=2 << 20,
    )
    middle = send(far, back(MIDDLE))
    handed = send(far, back(HANDED))
    own, onward = call(
        functools.partial(item_sums, (0, 1), 4),
        (shape(held, depth, dtype=F32), shape(held, depth, dtype=F32)),
        (adj_t, others_t, *shares, far),
        flops=3 * work // 4,
        nbytes=6 << 20,
    )
    near, new_users = call(
        functools.partial(item_sums_and, (2,), 4),
        (shape(held, depth), shape(share, depth, dtype=F32)),
        (adj_t, others_t, *shares, own, new_users),
        flops=work // 4,
        nbytes=2 << 20,
    )
    near = send(near, back(TURN_2))
    (onward,) = call(pass_on, (shape(held, depth),), (onward, handed), nbytes=1 << 19)
    new_items = pl.pallas_call(
        last_update,
        out_shape=shape(held, depth, dtype=F32),
        in_specs=[VMEM] * 7,
        out_specs=pl.BlockSpec(memory_space=pl.ANY),
        scratch_shapes=(pltpu.VMEM((held, depth), F32), pltpu.SemaphoreType.DMA((2,))),
        compiler_params=PARAMS,
        cost_estimate=pl.CostEstimate(flops=12 * held * depth * depth, bytes_accessed=4 << 20, transcendentals=0),
    )(item_emb, w_hi, w_lo, middle, own, near, send(onward, back(TURN_1)))
    return (new_users, new_items)


def gathered(n_au, n_ia, user_emb, item_emb, tiles, block_rows, block_cols, block_counts, w_self, w_inter):
    depth = w_self.shape[0]
    users, held = user_emb.shape[0], item_emb.shape[0]
    items = held * n_au
    share = users // n_ia
    work = 2 * users * items * depth

    blocks = lax.all_gather(item_emb.astype(BF16), "au", axis=0, tiled=True)
    (adj,) = call(
        functools.partial(dense, tiles.shape[2], False),
        (shape(users, items),),
        (block_rows, block_cols, block_counts, tiles),
        smem=3,
        nbytes=4 << 20,
    )
    (adj_t,) = call(functools.partial(flip, tiles.shape[2]), (shape(items, users),), (adj,), nbytes=4 << 20)
    w_hi, w_lo, own_emb = call(
        weights,
        (shape(2 * depth, depth), shape(2 * depth, depth), shape(share, depth, dtype=F32)),
        (user_emb, w_self, w_inter),
        nbytes=5 << 20,
    )
    (sums,) = call(
        user_sums, (shape(users, depth, dtype=F32),), (adj, blocks), flops=work, nbytes=6 << 20
    )
    sums = lax.psum_scatter(sums, "ia", scatter_dimension=0, tiled=True)
    new_users, user_half = call(
        functools.partial(update, 1),
        (shape(share, depth, dtype=F32), shape(share, depth)),
        (own_emb, w_hi, w_lo, sums),
        flops=12 * share * depth * depth,
        nbytes=3 << 20,
    )
    shares = lax.all_gather(user_half, "ia", axis=0, tiled=True)
    (sums,) = call(
        all_sums, (shape(items, depth, dtype=F32),), (adj_t, shares), flops=work, nbytes=6 << 20
    )
    sums = lax.psum_scatter(sums, "au", scatter_dimension=0, tiled=True)
    (new_items,) = call(
        functools.partial(update, 1),
        (shape(held, depth, dtype=F32),),
        (item_emb, w_hi, w_lo, sums),
        flops=12 * held * depth * depth,
        nbytes=4 << 20,
    )
    return (new_users, new_items)


def local(n_au, n_ia, user_emb, item_emb, tiles, *rest):
    edge = tiles.shape[2]
    if (n_au, n_ia) == (8, 4) and item_emb.shape[0] == edge and edge % (user_emb.shape[0] // n_ia) == 0:
        return in_turns(user_emb, item_emb, tiles, *rest)
    return gathered(n_au, n_ia, user_emb, item_emb, tiles, *rest)


def solution(mesh):
    in_specs = (
        P("au", None),
        P(("ia", "au"), None),
        P("au", "ia", None, None),
        P("au", "ia"),
        P("au", "ia"),
        P("au", "ia"),
        P(),
        P(),
    )
    out_specs = (P(("au", "ia"), None), P(("ia", "au"), None))
    return jax.shard_map(
        functools.partial(local, mesh.shape["au"], mesh.shape["ia"]),
        mesh=mesh,
        in_specs=in_specs,
        out_specs=out_specs,
        check_vma=False,
    )
```

```python
import functools

import jax
import jax.numpy as jnp
from jax import lax
from jax.experimental import pallas as pl
from jax.experimental.pallas import tpu as pltpu
from jax.sharding import PartitionSpec as P

F32 = jnp.float32
BF16 = jnp.bfloat16
VMEM = pl.BlockSpec(memory_space=pltpu.VMEM)
SMEM = pl.BlockSpec(memory_space=pltpu.SMEM)
PARAMS = pltpu.CompilerParams(vmem_limit_bytes=40 * 1024 * 1024)

TURN_1 = ((0, 2), (3, 1), (1, 0), (2, 3))
TURN_2 = ((0, 1), (3, 2), (1, 3), (2, 0))
MIDDLE = ((1, 2), (2, 1))
HANDED = ((2, 3), (1, 0), (3, 2), (0, 1))


def back(pairs):
    return tuple((b, a) for a, b in pairs)


def send(x, pairs):
    perm = [(2 * a + core, 2 * b + core) for a, b in pairs for core in (0, 1)]
    perm += [(i, i ^ 1) for i in range(8) if i // 2 not in [a for a, _ in pairs]]
    return lax.ppermute(x, "au", perm)


def swap(x, axis, n, by):
    return lax.ppermute(x, axis, [(i, i ^ by) for i in range(n)])


def slot_of(me, block):
    apart = block ^ me
    turn = apart >> 1
    swapped = in_middle() & ((turn == 1) | (turn == 2))
    return jnp.where(swapped, 3 - turn, turn) * 2 + (apart & 1)


def in_middle():
    z = lax.axis_index("au") >> 1
    return (z == 1) | (z == 2)


def call(kernel, out_shape, operands, smem=0, flops=0, nbytes=0):
    return pl.pallas_call(
        kernel,
        out_shape=out_shape,
        in_specs=[SMEM] * smem + [VMEM] * (len(operands) - smem),
        out_specs=jax.tree.map(lambda _: VMEM, out_shape),
        compiler_params=PARAMS,
        cost_estimate=pl.CostEstimate(flops=flops, bytes_accessed=nbytes, transcendentals=0),
    )(*operands)


def shape(*dims, dtype=BF16):
    return jax.ShapeDtypeStruct(dims, dtype)


def split(x):
    hi = x.astype(BF16)
    return hi, (x - hi.astype(F32)).astype(BF16)


def dot(a, b):
    return jnp.dot(a, b, preferred_element_type=F32)


def total(refs):
    value = refs[0][...].astype(F32)
    for ref in refs[1:]:
        value = value + ref[...].astype(F32)
    return value


def dense(piece, turns, rows, cols, count, tiles, adj):
    edge = tiles.shape[2]
    adj[...] = jnp.zeros_like(adj)

    def place(slot, carry):
        at = cols[0, slot]
        if turns:
            at = slot_of(lax.axis_index("au"), at)
        col = pl.multiple_of(at * edge, edge)
        for part in range(edge // piece):
            row = rows[0, slot] * (edge // piece) + part
            if turns:
                row = row ^ lax.axis_index("ia")
            row = pl.multiple_of(row * piece, piece)
            adj[pl.ds(row, piece), pl.ds(col, edge)] = tiles[0, slot, part * piece : (part + 1) * piece, :]
        return carry

    lax.fori_loop(0, count[0, 0], place, 0)


def flip(edge, adj, *outs):
    n = len(outs)
    for k in range(adj.shape[1] // edge):
        out = outs[k % n]
        out[k // n * edge : (k // n + 1) * edge, :] = adj[:, k * edge : (k + 1) * edge].T


def ready(edge, adj, user_emb, w_self, w_inter, w_hi, w_lo, own, *adj_t):
    weights(user_emb, w_self, w_inter, w_hi, w_lo, own)
    flip(edge, adj, *adj_t)


def weights(user_emb, w_self, w_inter, w_hi, w_lo, own):
    depth = w_self.shape[0]
    for k, w in enumerate((w_self, w_inter)):
        w_hi[k * depth : (k + 1) * depth, :], w_lo[k * depth : (k + 1) * depth, :] = split(w[...])
    height = own.shape[0]
    own[...] = user_emb[pl.ds(pl.multiple_of(lax.axis_index("ia") * height, height), height), :]


def block_sums(adj, first, blocks):
    edge = blocks[0].shape[0]
    return sum(dot(adj[:, (first + k) * edge : (first + k + 1) * edge], block) for k, block in enumerate(blocks))


def early_sums(adj, *refs):
    *blocks, middle, ends, sums = refs
    blocks = [block[...] for block in blocks] + [jnp.where(in_middle(), middle[...], ends[...])]
    sums[...] = block_sums(adj, 0, blocks)


def late_sums(adj, early, middle, ends, *outs):
    sums = early[...] + block_sums(adj, 7, [jnp.where(in_middle(), middle[...], ends[...])])
    height = outs[0].shape[0]
    for k, out in enumerate(outs):
        out[...] = sums[k * height : (k + 1) * height].astype(out.dtype)


def user_sums(adj, items, out):
    out[...] = dot(adj[...], items[...])


def item_sums(slots, n, *refs):
    adj_t, shares, outs = refs[:2], refs[2 : 2 + 2 * n], refs[-len(slots) :]
    users = [jnp.concatenate([share[...] for share in shares[core * n : core * n + n]], axis=0) for core in (0, 1)]
    edge = outs[0].shape[0]
    for slot, out in zip(slots, outs):
        rows = slice(slot * edge, (slot + 1) * edge)
        out[...] = (dot(adj_t[0][rows, :], users[0]) + dot(adj_t[1][rows, :], users[1])).astype(out.dtype)


def item_sums_and(starts, n, *refs):
    refs[-1][...] = refs[-len(starts) - 2][...]
    item_sums(starts, n, *refs[: -len(starts) - 2], *refs[-len(starts) - 1 : -1])


def all_sums(adj_t, users, out):
    out[...] = dot(adj_t[...], users[...])


def pass_on(sums, handed, out):
    given = jnp.where(in_middle(), handed[...].astype(F32), 0)
    out[...] = (sums[...] + given).astype(out.dtype)


def mix(side, own, w_hi, w_lo):
    height = own.shape[0]
    hi, lo = split(jnp.concatenate([side + own, side * own], axis=1))
    both = dot(jnp.concatenate([hi, lo], axis=0), w_hi)
    mixed = both[:height] + (both[height:] + dot(hi, w_lo))
    return jnp.where(mixed >= 0, mixed, 0.2 * mixed)


def update(n, emb, w_hi, w_lo, *refs):
    mixed = mix(total(refs[:n]), emb[...], w_hi[...], w_lo[...])
    for out in refs[n:]:
        out[...] = mixed.astype(out.dtype)


def arrived(own, near, middle, out):
    out[...] = own[...] + near[...].astype(F32) + jnp.where(in_middle(), middle[...].astype(F32), 0)


def last_update(emb, w_hi, w_lo, sums, onward, out, ready, sems):
    n = sems.shape[0]
    copies = []
    for k in range(n):
        rows = slice(k * (out.shape[0] // n), (k + 1) * (out.shape[0] // n))
        side = sums[rows, :] + onward[rows, :].astype(F32)
        ready[rows, :] = mix(side, emb[rows, :], w_hi[...], w_lo[...])
        copies.append(pltpu.make_async_copy(ready.at[rows, :], out.at[rows, :], sems.at[k]))
        copies[k].start()
    for copy in copies:
        copy.wait()


def in_turns(user_emb, item_emb, tiles, block_rows, block_cols, block_counts, w_self, w_inter):
    depth = w_self.shape[0]
    users, held = user_emb.shape[0], item_emb.shape[0]
    items = held * 8
    share = users // 4
    work = 2 * users * items * depth

    def other(x):
        return swap(x, "au", 8, 1)

    def after(x, *done):
        return lax.optimization_barrier((x, *done))[0]

    mine = item_emb.astype(BF16)
    first = send(mine, TURN_1)
    (adj,) = call(
        functools.partial(dense, share, True),
        (shape(users, items),),
        (block_rows, block_cols, block_counts, tiles),
        smem=3,
        nbytes=8 << 20,
    )
    second = send(after(mine, adj), TURN_2)
    w_hi, w_lo, own_emb, adj_t, others_t = call(
        functools.partial(ready, held),
        (shape(2 * depth, depth), shape(2 * depth, depth), shape(share, depth, dtype=F32))
        + (shape(items // 2, users), shape(items // 2, users)),
        (adj, user_emb, w_self, w_inter),
        nbytes=9 << 20,
    )
    middle = send(after(mine, w_hi), MIDDLE)
    first = after(first, w_hi)
    ends = send(first, HANDED)
    (early,) = call(
        early_sums,
        (shape(users, depth, dtype=F32),),
        (adj, mine, other(mine), first, other(first), second, other(second), middle, ends),
        flops=work // 2,
        nbytes=4 << 20,
    )
    own, *others = call(
        late_sums,
        (shape(share, depth, dtype=F32),) + (shape(share, depth),) * 3,
        (adj, early, other(middle), other(ends)),
        flops=work // 2,
        nbytes=4 << 20,
    )
    others_t = other(after(others_t, own))
    own = after(own, others_t)
    new_users, user_half = call(
        functools.partial(update, 4),
        (shape(share, depth, dtype=F32), shape(share, depth)),
        (own_emb, w_hi, w_lo, *(swap(others[k - 1], "ia", 4, k) for k in (1, 2, 3)), own),
        flops=12 * share * depth * depth,
        nbytes=3 << 20,
    )

    shares = [user_half] + [swap(user_half, "ia", 4, k) for k in (1, 2, 3)]
    shares[1:3] = lax.optimization_barrier(tuple(shares[1:3]))
    shares += [other(x) for x in shares]
    (far,) = call(
        functools.partial(item_sums, (3,), 4),
        (shape(held, depth),),
        (adj_t, others_t, *shares),
        flops=work // 4,
        nbytes=2 << 20,
    )
    middle = send(far, back(MIDDLE))
    handed = send(far, back(HANDED))
    own, onward = call(
        functools.partial(item_sums, (0, 1), 4),
        (shape(held, depth, dtype=F32), shape(held, depth, dtype=F32)),
        (adj_t, others_t, *shares, far),
        flops=3 * work // 4,
        nbytes=6 << 20,
    )
    near, new_users = call(
        functools.partial(item_sums_and, (2,), 4),
        (shape(held, depth), shape(share, depth, dtype=F32)),
        (adj_t, others_t, *shares, own, new_users),
        flops=work // 4,
        nbytes=2 << 20,
    )
    near = send(near, back(TURN_2))
    (onward,) = call(pass_on, (shape(held, depth),), (onward, handed), nbytes=1 << 19)
    (own,) = call(arrived, (shape(held, depth, dtype=F32),), (own, near, middle), nbytes=1 << 20)
    new_items = pl.pallas_call(
        last_update,
        out_shape=shape(held, depth, dtype=F32),
        in_specs=[VMEM] * 5,
        out_specs=pl.BlockSpec(memory_space=pl.ANY),
        scratch_shapes=(pltpu.VMEM((held, depth), F32), pltpu.SemaphoreType.DMA((2,))),
        compiler_params=PARAMS,
        cost_estimate=pl.CostEstimate(flops=12 * held * depth * depth, bytes_accessed=4 << 20, transcendentals=0),
    )(item_emb, w_hi, w_lo, own, send(onward, back(TURN_1)))
    return (new_users, new_items)


def gathered(n_au, n_ia, user_emb, item_emb, tiles, block_rows, block_cols, block_counts, w_self, w_inter):
    depth = w_self.shape[0]
    users, held = user_emb.shape[0], item_emb.shape[0]
    items = held * n_au
    share = users // n_ia
    work = 2 * users * items * depth

    blocks = lax.all_gather(item_emb.astype(BF16), "au", axis=0, tiled=True)
    (adj,) = call(
        functools.partial(dense, tiles.shape[2], False),
        (shape(users, items),),
        (block_rows, block_cols, block_counts, tiles),
        smem=3,
        nbytes=4 << 20,
    )
    (adj_t,) = call(functools.partial(flip, tiles.shape[2]), (shape(items, users),), (adj,), nbytes=4 << 20)
    w_hi, w_lo, own_emb = call(
        weights,
        (shape(2 * depth, depth), shape(2 * depth, depth), shape(share, depth, dtype=F32)),
        (user_emb, w_self, w_inter),
        nbytes=5 << 20,
    )
    (sums,) = call(
        user_sums, (shape(users, depth, dtype=F32),), (adj, blocks), flops=work, nbytes=6 << 20
    )
    sums = lax.psum_scatter(sums, "ia", scatter_dimension=0, tiled=True)
    new_users, user_half = call(
        functools.partial(update, 1),
        (shape(share, depth, dtype=F32), shape(share, depth)),
        (own_emb, w_hi, w_lo, sums),
        flops=12 * share * depth * depth,
        nbytes=3 << 20,
    )
    shares = lax.all_gather(user_half, "ia", axis=0, tiled=True)
    (sums,) = call(
        all_sums, (shape(items, depth, dtype=F32),), (adj_t, shares), flops=work, nbytes=6 << 20
    )
    sums = lax.psum_scatter(sums, "au", scatter_dimension=0, tiled=True)
    (new_items,) = call(
        functools.partial(update, 1),
        (shape(held, depth, dtype=F32),),
        (item_emb, w_hi, w_lo, sums),
        flops=12 * held * depth * depth,
        nbytes=4 << 20,
    )
    return (new_users, new_items)


def local(n_au, n_ia, user_emb, item_emb, tiles, *rest):
    edge = tiles.shape[2]
    if (n_au, n_ia) == (8, 4) and item_emb.shape[0] == edge and edge % (user_emb.shape[0] // n_ia) == 0:
        return in_turns(user_emb, item_emb, tiles, *rest)
    return gathered(n_au, n_ia, user_emb, item_emb, tiles, *rest)


def solution(mesh):
    in_specs = (
        P("au", None),
        P(("ia", "au"), None),
        P("au", "ia", None, None),
        P("au", "ia"),
        P("au", "ia"),
        P("au", "ia"),
        P(),
        P(),
    )
    out_specs = (P(("au", "ia"), None), P(("ia", "au"), None))
    return jax.shard_map(
        functools.partial(local, mesh.shape["au"], mesh.shape["ia"]),
        mesh=mesh,
        in_specs=in_specs,
        out_specs=out_specs,
        check_vma=False,
    )
```

```python
import functools

import jax
import jax.numpy as jnp
from jax import lax
from jax.experimental import pallas as pl
from jax.experimental.pallas import tpu as pltpu
from jax.sharding import PartitionSpec as P

F32 = jnp.float32
BF16 = jnp.bfloat16
VMEM = pl.BlockSpec(memory_space=pltpu.VMEM)
SMEM = pl.BlockSpec(memory_space=pltpu.SMEM)
PARAMS = pltpu.CompilerParams(vmem_limit_bytes=40 * 1024 * 1024)

TURN_1 = ((0, 2), (3, 1), (1, 0), (2, 3))
TURN_2 = ((0, 1), (3, 2), (1, 3), (2, 0))
MIDDLE = ((1, 2), (2, 1))
HANDED = ((2, 3), (1, 0), (3, 2), (0, 1))


def back(pairs):
    return tuple((b, a) for a, b in pairs)


def send(x, pairs):
    perm = [(2 * a + core, 2 * b + core) for a, b in pairs for core in (0, 1)]
    perm += [(i, i ^ 1) for i in range(8) if i // 2 not in [a for a, _ in pairs]]
    return lax.ppermute(x, "au", perm)


def swap(x, axis, n, by):
    return lax.ppermute(x, axis, [(i, i ^ by) for i in range(n)])


def slot_of(me, block):
    apart = block ^ me
    turn = apart >> 1
    swapped = in_middle() & ((turn == 1) | (turn == 2))
    return jnp.where(swapped, 3 - turn, turn) * 2 + (apart & 1)


def in_middle():
    z = lax.axis_index("au") >> 1
    return (z == 1) | (z == 2)


def call(kernel, out_shape, operands, smem=0, flops=0, nbytes=0):
    return pl.pallas_call(
        kernel,
        out_shape=out_shape,
        in_specs=[SMEM] * smem + [VMEM] * (len(operands) - smem),
        out_specs=jax.tree.map(lambda _: VMEM, out_shape),
        compiler_params=PARAMS,
        cost_estimate=pl.CostEstimate(flops=flops, bytes_accessed=nbytes, transcendentals=0),
    )(*operands)


def shape(*dims, dtype=BF16):
    return jax.ShapeDtypeStruct(dims, dtype)


def split(x):
    hi = x.astype(BF16)
    return hi, (x - hi.astype(F32)).astype(BF16)


def dot(a, b):
    return jnp.dot(a, b, preferred_element_type=F32)


def total(refs):
    value = refs[0][...].astype(F32)
    for ref in refs[1:]:
        value = value + ref[...].astype(F32)
    return value


def dense(piece, turns, rows, cols, count, tiles, adj):
    edge = tiles.shape[2]
    adj[...] = jnp.zeros_like(adj)

    def place(slot, carry):
        at = cols[0, slot]
        if turns:
            at = slot_of(lax.axis_index("au"), at)
        col = pl.multiple_of(at * edge, edge)
        for part in range(edge // piece):
            row = rows[0, slot] * (edge // piece) + part
            if turns:
                row = row ^ lax.axis_index("ia")
            row = pl.multiple_of(row * piece, piece)
            adj[pl.ds(row, piece), pl.ds(col, edge)] = tiles[0, slot, part * piece : (part + 1) * piece, :]
        return carry

    lax.fori_loop(0, count[0, 0], place, 0)


def flip(edge, adj, *outs):
    n = len(outs)
    for k in range(adj.shape[1] // edge):
        out = outs[k % n]
        out[k // n * edge : (k // n + 1) * edge, :] = adj[:, k * edge : (k + 1) * edge].T


def ready(edge, adj, user_emb, w_self, w_inter, w_hi, w_lo, own, *adj_t):
    weights(user_emb, w_self, w_inter, w_hi, w_lo, own)
    flip(edge, adj, *adj_t)


def weights(user_emb, w_self, w_inter, w_hi, w_lo, own):
    depth = w_self.shape[0]
    for k, w in enumerate((w_self, w_inter)):
        w_hi[k * depth : (k + 1) * depth, :], w_lo[k * depth : (k + 1) * depth, :] = split(w[...])
    height = own.shape[0]
    own[...] = user_emb[pl.ds(pl.multiple_of(lax.axis_index("ia") * height, height), height), :]


def block_sums(adj, first, blocks):
    edge = blocks[0].shape[0]
    return sum(dot(adj[:, (first + k) * edge : (first + k + 1) * edge], block) for k, block in enumerate(blocks))


def early_sums(adj, *refs):
    *blocks, middle, ends, sums = refs
    blocks = [block[...] for block in blocks] + [jnp.where(in_middle(), middle[...], ends[...])]
    sums[...] = block_sums(adj, 0, blocks)


def late_sums(adj, early, middle, ends, *outs):
    sums = early[...] + block_sums(adj, 7, [jnp.where(in_middle(), middle[...], ends[...])])
    height = outs[0].shape[0]
    for k, out in enumerate(outs):
        out[...] = sums[k * height : (k + 1) * height].astype(out.dtype)


def user_sums(adj, items, out):
    out[...] = dot(adj[...], items[...])


def item_sums(slots, n, *refs):
    adj_t, shares, outs = refs[:2], refs[2 : 2 + 2 * n], refs[-len(slots) :]
    users = [jnp.concatenate([share[...] for share in shares[core * n : core * n + n]], axis=0) for core in (0, 1)]
    edge = outs[0].shape[0]
    for slot, out in zip(slots, outs):
        rows = slice(slot * edge, (slot + 1) * edge)
        out[...] = (dot(adj_t[0][rows, :], users[0]) + dot(adj_t[1][rows, :], users[1])).astype(out.dtype)


def item_sums_and(starts, n, *refs):
    refs[-1][...] = refs[-len(starts) - 2][...]
    item_sums(starts, n, *refs[: -len(starts) - 2], *refs[-len(starts) - 1 : -1])


def all_sums(adj_t, users, out):
    out[...] = dot(adj_t[...], users[...])


def pass_on(sums, handed, out):
    given = jnp.where(in_middle(), handed[...].astype(F32), 0)
    out[...] = (sums[...] + given).astype(out.dtype)


def mix(side, own, w_hi, w_lo):
    height = own.shape[0]
    hi, lo = split(jnp.concatenate([side + own, side * own], axis=1))
    both = dot(jnp.concatenate([hi, lo], axis=0), w_hi)
    mixed = both[:height] + (both[height:] + dot(hi, w_lo))
    return jnp.where(mixed >= 0, mixed, 0.2 * mixed)


def update(n, emb, w_hi, w_lo, *refs):
    mixed = mix(total(refs[:n]), emb[...], w_hi[...], w_lo[...])
    for out in refs[n:]:
        out[...] = mixed.astype(out.dtype)


def last_update(emb, w_hi, w_lo, middle, own, near, onward, out, ready, sems):
    inner = in_middle()
    n = sems.shape[0]
    copies = []
    for k in range(n):
        rows = slice(k * (out.shape[0] // n), (k + 1) * (out.shape[0] // n))
        side = own[rows, :] + near[rows, :].astype(F32) + onward[rows, :].astype(F32)
        side = side + jnp.where(inner, middle[rows, :].astype(F32), 0)
        ready[rows, :] = mix(side, emb[rows, :], w_hi[...], w_lo[...])
        copies.append(pltpu.make_async_copy(ready.at[rows, :], out.at[rows, :], sems.at[k]))
        copies[k].start()
    for copy in copies:
        copy.wait()


def in_turns(user_emb, item_emb, tiles, block_rows, block_cols, block_counts, w_self, w_inter):
    depth = w_self.shape[0]
    users, held = user_emb.shape[0], item_emb.shape[0]
    items = held * 8
    share = users // 4
    work = 2 * users * items * depth

    def other(x):
        return swap(x, "au", 8, 1)

    def after(x, *done):
        return lax.optimization_barrier((x, *done))[0]

    mine = item_emb.astype(BF16)
    first = send(mine, TURN_1)
    (adj,) = call(
        functools.partial(dense, share, True),
        (shape(users, items),),
        (block_rows, block_cols, block_counts, tiles),
        smem=3,
        nbytes=8 << 20,
    )
    second = send(after(mine, adj), TURN_2)
    w_hi, w_lo, own_emb, adj_t, others_t = call(
        functools.partial(ready, held),
        (shape(2 * depth, depth), shape(2 * depth, depth), shape(share, depth, dtype=F32))
        + (shape(items // 2, users), shape(items // 2, users)),
        (adj, user_emb, w_self, w_inter),
        nbytes=9 << 20,
    )
    middle = send(after(mine, w_hi), MIDDLE)
    first = after(first, w_hi)
    ends = lax.ppermute(first, "au", [(2 * a + core, 2 * b + core) for a, b in HANDED[:2] for core in (0, 1)])
    (early,) = call(
        early_sums,
        (shape(users, depth, dtype=F32),),
        (adj, mine, other(mine), first, other(first), second, other(second), middle, ends),
        flops=work // 2,
        nbytes=4 << 20,
    )
    own, *others = call(
        late_sums,
        (shape(share, depth, dtype=F32),) + (shape(share, depth),) * 3,
        (adj, early, other(middle), other(ends)),
        flops=work // 2,
        nbytes=4 << 20,
    )
    others_t = other(after(others_t, own))
    own = after(own, others_t)
    new_users, user_half = call(
        functools.partial(update, 4),
        (shape(share, depth, dtype=F32), shape(share, depth)),
        (own_emb, w_hi, w_lo, *(swap(others[k - 1], "ia", 4, k) for k in (1, 2, 3)), own),
        flops=12 * share * depth * depth,
        nbytes=3 << 20,
    )

    shares = [user_half] + [swap(user_half, "ia", 4, k) for k in (1, 2, 3)]
    shares[1:3] = lax.optimization_barrier(tuple(shares[1:3]))
    shares += [other(x) for x in shares]
    (far,) = call(
        functools.partial(item_sums, (3,), 4),
        (shape(held, depth),),
        (adj_t, others_t, *shares),
        flops=work // 4,
        nbytes=2 << 20,
    )
    middle = send(far, back(MIDDLE))
    handed = send(far, back(HANDED))
    own, onward = call(
        functools.partial(item_sums, (0, 1), 4),
        (shape(held, depth, dtype=F32), shape(held, depth, dtype=F32)),
        (adj_t, others_t, *shares, far),
        flops=3 * work // 4,
        nbytes=6 << 20,
    )
    near, new_users = call(
        functools.partial(item_sums_and, (2,), 4),
        (shape(held, depth), shape(share, depth, dtype=F32)),
        (adj_t, others_t, *shares, own, new_users),
        flops=work // 4,
        nbytes=2 << 20,
    )
    near = send(near, back(TURN_2))
    (onward,) = call(pass_on, (shape(held, depth),), (onward, handed), nbytes=1 << 19)
    new_items = pl.pallas_call(
        last_update,
        out_shape=shape(held, depth, dtype=F32),
        in_specs=[VMEM] * 7,
        out_specs=pl.BlockSpec(memory_space=pl.ANY),
        scratch_shapes=(pltpu.VMEM((held, depth), F32), pltpu.SemaphoreType.DMA((2,))),
        compiler_params=PARAMS,
        cost_estimate=pl.CostEstimate(flops=12 * held * depth * depth, bytes_accessed=4 << 20, transcendentals=0),
    )(item_emb, w_hi, w_lo, middle, own, near, send(onward, back(TURN_1)))
    return (new_users, new_items)


def gathered(n_au, n_ia, user_emb, item_emb, tiles, block_rows, block_cols, block_counts, w_self, w_inter):
    depth = w_self.shape[0]
    users, held = user_emb.shape[0], item_emb.shape[0]
    items = held * n_au
    share = users // n_ia
    work = 2 * users * items * depth

    blocks = lax.all_gather(item_emb.astype(BF16), "au", axis=0, tiled=True)
    (adj,) = call(
        functools.partial(dense, tiles.shape[2], False),
        (shape(users, items),),
        (block_rows, block_cols, block_counts, tiles),
        smem=3,
        nbytes=4 << 20,
    )
    (adj_t,) = call(functools.partial(flip, tiles.shape[2]), (shape(items, users),), (adj,), nbytes=4 << 20)
    w_hi, w_lo, own_emb = call(
        weights,
        (shape(2 * depth, depth), shape(2 * depth, depth), shape(share, depth, dtype=F32)),
        (user_emb, w_self, w_inter),
        nbytes=5 << 20,
    )
    (sums,) = call(
        user_sums, (shape(users, depth, dtype=F32),), (adj, blocks), flops=work, nbytes=6 << 20
    )
    sums = lax.psum_scatter(sums, "ia", scatter_dimension=0, tiled=True)
    new_users, user_half = call(
        functools.partial(update, 1),
        (shape(share, depth, dtype=F32), shape(share, depth)),
        (own_emb, w_hi, w_lo, sums),
        flops=12 * share * depth * depth,
        nbytes=3 << 20,
    )
    shares = lax.all_gather(user_half, "ia", axis=0, tiled=True)
    (sums,) = call(
        all_sums, (shape(items, depth, dtype=F32),), (adj_t, shares), flops=work, nbytes=6 << 20
    )
    sums = lax.psum_scatter(sums, "au", scatter_dimension=0, tiled=True)
    (new_items,) = call(
        functools.partial(update, 1),
        (shape(held, depth, dtype=F32),),
        (item_emb, w_hi, w_lo, sums),
        flops=12 * held * depth * depth,
        nbytes=4 << 20,
    )
    return (new_users, new_items)


def local(n_au, n_ia, user_emb, item_emb, tiles, *rest):
    edge = tiles.shape[2]
    if (n_au, n_ia) == (8, 4) and item_emb.shape[0] == edge and edge % (user_emb.shape[0] // n_ia) == 0:
        return in_turns(user_emb, item_emb, tiles, *rest)
    return gathered(n_au, n_ia, user_emb, item_emb, tiles, *rest)


def solution(mesh):
    in_specs = (
        P("au", None),
        P(("ia", "au"), None),
        P("au", "ia", None, None),
        P("au", "ia"),
        P("au", "ia"),
        P("au", "ia"),
        P(),
        P(),
    )
    out_specs = (P(("au", "ia"), None), P(("ia", "au"), None))
    return jax.shard_map(
        functools.partial(local, mesh.shape["au"], mesh.shape["ia"]),
        mesh=mesh,
        in_specs=in_specs,
        out_specs=out_specs,
        check_vma=False,
    )
```

```python
import functools

import jax
import jax.numpy as jnp
from jax import lax
from jax.experimental import pallas as pl
from jax.experimental.pallas import tpu as pltpu
from jax.sharding import PartitionSpec as P

F32 = jnp.float32
BF16 = jnp.bfloat16
VMEM = pl.BlockSpec(memory_space=pltpu.VMEM)
SMEM = pl.BlockSpec(memory_space=pltpu.SMEM)
PARAMS = pltpu.CompilerParams(vmem_limit_bytes=40 * 1024 * 1024)

TURN_1 = ((0, 2), (3, 1), (1, 0), (2, 3))
TURN_2 = ((0, 1), (3, 2), (1, 3), (2, 0))
MIDDLE = ((1, 2), (2, 1))
HANDED = ((2, 3), (1, 0), (3, 2), (0, 1))


def back(pairs):
    return tuple((b, a) for a, b in pairs)


def send(x, pairs):
    perm = [(2 * a + core, 2 * b + core) for a, b in pairs for core in (0, 1)]
    perm += [(i, i ^ 1) for i in range(8) if i // 2 not in [a for a, _ in pairs]]
    return lax.ppermute(x, "au", perm)


def swap(x, axis, n, by):
    return lax.ppermute(x, axis, [(i, i ^ by) for i in range(n)])


def slot_of(me, block):
    apart = block ^ me
    turn = apart >> 1
    swapped = in_middle() & ((turn == 1) | (turn == 2))
    return jnp.where(swapped, 3 - turn, turn) * 2 + (apart & 1)


def in_middle():
    z = lax.axis_index("au") >> 1
    return (z == 1) | (z == 2)


def call(kernel, out_shape, operands, smem=0, flops=0, nbytes=0):
    return pl.pallas_call(
        kernel,
        out_shape=out_shape,
        in_specs=[SMEM] * smem + [VMEM] * (len(operands) - smem),
        out_specs=jax.tree.map(lambda _: VMEM, out_shape),
        compiler_params=PARAMS,
        cost_estimate=pl.CostEstimate(flops=flops, bytes_accessed=nbytes, transcendentals=0),
    )(*operands)


def shape(*dims, dtype=BF16):
    return jax.ShapeDtypeStruct(dims, dtype)


def split(x):
    hi = x.astype(BF16)
    return hi, (x - hi.astype(F32)).astype(BF16)


def dot(a, b):
    return jnp.dot(a, b, preferred_element_type=F32)


def total(refs):
    value = refs[0][...].astype(F32)
    for ref in refs[1:]:
        value = value + ref[...].astype(F32)
    return value


def dense(piece, turns, rows, cols, count, tiles, adj):
    edge = tiles.shape[2]
    adj[...] = jnp.zeros_like(adj)

    def place(slot, carry):
        at = cols[0, slot]
        if turns:
            at = slot_of(lax.axis_index("au"), at)
        col = pl.multiple_of(at * edge, edge)
        for part in range(edge // piece):
            row = rows[0, slot] * (edge // piece) + part
            if turns:
                row = row ^ lax.axis_index("ia")
            row = pl.multiple_of(row * piece, piece)
            adj[pl.ds(row, piece), pl.ds(col, edge)] = tiles[0, slot, part * piece : (part + 1) * piece, :]
        return carry

    lax.fori_loop(0, count[0, 0], place, 0)


def flip(edge, adj, *outs):
    n = len(outs)
    for k in range(adj.shape[1] // edge):
        out = outs[k % n]
        out[k // n * edge : (k // n + 1) * edge, :] = adj[:, k * edge : (k + 1) * edge].T


def ready(edge, adj, user_emb, w_self, w_inter, w_hi, w_lo, own, *adj_t):
    weights(user_emb, w_self, w_inter, w_hi, w_lo, own)
    flip(edge, adj, *adj_t)


def weights(user_emb, w_self, w_inter, w_hi, w_lo, own):
    depth = w_self.shape[0]
    for k, w in enumerate((w_self, w_inter)):
        w_hi[k * depth : (k + 1) * depth, :], w_lo[k * depth : (k + 1) * depth, :] = split(w[...])
    height = own.shape[0]
    own[...] = user_emb[pl.ds(pl.multiple_of(lax.axis_index("ia") * height, height), height), :]


def block_sums(adj, first, blocks):
    edge = blocks[0].shape[0]
    return sum(dot(adj[:, (first + k) * edge : (first + k + 1) * edge], block) for k, block in enumerate(blocks))


def early_sums(adj, *refs):
    *blocks, middle, ends, sums = refs
    blocks = [block[...] for block in blocks] + [jnp.where(in_middle(), middle[...], ends[...])]
    sums[...] = block_sums(adj, 0, blocks)


def late_sums(adj, early, middle, ends, *outs):
    sums = early[...] + block_sums(adj, 7, [jnp.where(in_middle(), middle[...], ends[...])])
    height = outs[0].shape[0]
    for k, out in enumerate(outs):
        out[...] = sums[k * height : (k + 1) * height].astype(out.dtype)


def user_sums(adj, items, out):
    out[...] = dot(adj[...], items[...])


def item_sums(slots, n, *refs):
    adj_t, shares, outs = refs[:2], refs[2 : 2 + 2 * n], refs[-len(slots) :]
    users = [jnp.concatenate([share[...] for share in shares[core * n : core * n + n]], axis=0) for core in (0, 1)]
    edge = outs[0].shape[0]
    for slot, out in zip(slots, outs):
        rows = slice(slot * edge, (slot + 1) * edge)
        out[...] = (dot(adj_t[0][rows, :], users[0]) + dot(adj_t[1][rows, :], users[1])).astype(out.dtype)


def item_sums_and(starts, n, *refs):
    refs[-1][...] = refs[-len(starts) - 2][...]
    item_sums(starts, n, *refs[: -len(starts) - 2], *refs[-len(starts) - 1 : -1])


def all_sums(adj_t, users, out):
    out[...] = dot(adj_t[...], users[...])


def pass_on(sums, handed, out):
    given = jnp.where(in_middle(), handed[...].astype(F32), 0)
    out[...] = (sums[...] + given).astype(out.dtype)


def mix(side, own, w_hi, w_lo):
    height = own.shape[0]
    hi, lo = split(jnp.concatenate([side + own, side * own], axis=1))
    both = dot(jnp.concatenate([hi, lo], axis=0), w_hi)
    mixed = both[:height] + (both[height:] + dot(hi, w_lo))
    return jnp.where(mixed >= 0, mixed, 0.2 * mixed)


def update(n, emb, w_hi, w_lo, *refs):
    mixed = mix(total(refs[:n]), emb[...], w_hi[...], w_lo[...])
    for out in refs[n:]:
        out[...] = mixed.astype(out.dtype)


def last_update(emb, w_hi, w_lo, middle, own, near, onward, out, ready, sems):
    inner = in_middle()
    n = sems.shape[0]
    copies = []
    for k in range(n):
        rows = slice(k * (out.shape[0] // n), (k + 1) * (out.shape[0] // n))
        side = own[rows, :] + near[rows, :].astype(F32) + onward[rows, :].astype(F32)
        side = side + jnp.where(inner, middle[rows, :].astype(F32), 0)
        ready[rows, :] = mix(side, emb[rows, :], w_hi[...], w_lo[...])
        copies.append(pltpu.make_async_copy(ready.at[rows, :], out.at[rows, :], sems.at[k]))
        copies[k].start()
    for copy in copies:
        copy.wait()


def in_turns(user_emb, item_emb, tiles, block_rows, block_cols, block_counts, w_self, w_inter):
    depth = w_self.shape[0]
    users, held = user_emb.shape[0], item_emb.shape[0]
    items = held * 8
    share = users // 4
    work = 2 * users * items * depth

    def other(x):
        return swap(x, "au", 8, 1)

    def after(x, *done):
        return lax.optimization_barrier((x, *done))[0]

    mine = item_emb.astype(BF16)
    first = send(mine, TURN_1)
    (adj,) = call(
        functools.partial(dense, share, True),
        (shape(users, items),),
        (block_rows, block_cols, block_counts, tiles),
        smem=3,
        nbytes=8 << 20,
    )
    second = send(after(mine, adj), TURN_2)
    w_hi, w_lo, own_emb, adj_t, others_t = call(
        functools.partial(ready, held),
        (shape(2 * depth, depth), shape(2 * depth, depth), shape(share, depth, dtype=F32))
        + (shape(items // 2, users), shape(items // 2, users)),
        (adj, user_emb, w_self, w_inter),
        nbytes=9 << 20,
    )
    middle = send(after(mine, w_hi), MIDDLE)
    first = after(first, w_hi)
    ends = lax.ppermute(first, "au", [(2 * a + core, 2 * b + core) for a, b in HANDED[:2] for core in (0, 1)])
    (early,) = call(
        early_sums,
        (shape(users, depth, dtype=F32),),
        (adj, mine, other(mine), first, other(first), second, other(second), middle, ends),
        flops=work // 2,
        nbytes=4 << 20,
    )
    own, *others = call(
        late_sums,
        (shape(share, depth, dtype=F32),) + (shape(share, depth),) * 3,
        (adj, early, other(middle), other(ends)),
        flops=work // 2,
        nbytes=4 << 20,
    )
    new_users, user_half = call(
        functools.partial(update, 4),
        (shape(share, depth, dtype=F32), shape(share, depth)),
        (own_emb, w_hi, w_lo, *(swap(others[k - 1], "ia", 4, k) for k in (1, 2, 3)), own),
        flops=12 * share * depth * depth,
        nbytes=3 << 20,
    )

    others_t = other(after(others_t, user_half))
    shares = [user_half] + [swap(user_half, "ia", 4, k) for k in (1, 2, 3)]
    shares[1:3] = lax.optimization_barrier(tuple(shares[1:3]))
    shares += [other(x) for x in shares]
    (far,) = call(
        functools.partial(item_sums, (3,), 4),
        (shape(held, depth),),
        (adj_t, others_t, *shares),
        flops=work // 4,
        nbytes=2 << 20,
    )
    middle = send(far, back(MIDDLE))
    handed = send(far, back(HANDED))
    own, onward = call(
        functools.partial(item_sums, (0, 1), 4),
        (shape(held, depth, dtype=F32), shape(held, depth, dtype=F32)),
        (adj_t, others_t, *shares, far),
        flops=3 * work // 4,
        nbytes=6 << 20,
    )
    near, new_users = call(
        functools.partial(item_sums_and, (2,), 4),
        (shape(held, depth), shape(share, depth, dtype=F32)),
        (adj_t, others_t, *shares, own, new_users),
        flops=work // 4,
        nbytes=2 << 20,
    )
    near = send(near, back(TURN_2))
    (onward,) = call(pass_on, (shape(held, depth),), (onward, handed), nbytes=1 << 19)
    new_items = pl.pallas_call(
        last_update,
        out_shape=shape(held, depth, dtype=F32),
        in_specs=[VMEM] * 7,
        out_specs=pl.BlockSpec(memory_space=pl.ANY),
        scratch_shapes=(pltpu.VMEM((held, depth), F32), pltpu.SemaphoreType.DMA((2,))),
        compiler_params=PARAMS,
        cost_estimate=pl.CostEstimate(flops=12 * held * depth * depth, bytes_accessed=4 << 20, transcendentals=0),
    )(item_emb, w_hi, w_lo, middle, own, near, send(onward, back(TURN_1)))
    return (new_users, new_items)


def gathered(n_au, n_ia, user_emb, item_emb, tiles, block_rows, block_cols, block_counts, w_self, w_inter):
    depth = w_self.shape[0]
    users, held = user_emb.shape[0], item_emb.shape[0]
    items = held * n_au
    share = users // n_ia
    work = 2 * users * items * depth

    blocks = lax.all_gather(item_emb.astype(BF16), "au", axis=0, tiled=True)
    (adj,) = call(
        functools.partial(dense, tiles.shape[2], False),
        (shape(users, items),),
        (block_rows, block_cols, block_counts, tiles),
        smem=3,
        nbytes=4 << 20,
    )
    (adj_t,) = call(functools.partial(flip, tiles.shape[2]), (shape(items, users),), (adj,), nbytes=4 << 20)
    w_hi, w_lo, own_emb = call(
        weights,
        (shape(2 * depth, depth), shape(2 * depth, depth), shape(share, depth, dtype=F32)),
        (user_emb, w_self, w_inter),
        nbytes=5 << 20,
    )
    (sums,) = call(
        user_sums, (shape(users, depth, dtype=F32),), (adj, blocks), flops=work, nbytes=6 << 20
    )
    sums = lax.psum_scatter(sums, "ia", scatter_dimension=0, tiled=True)
    new_users, user_half = call(
        functools.partial(update, 1),
        (shape(share, depth, dtype=F32), shape(share, depth)),
        (own_emb, w_hi, w_lo, sums),
        flops=12 * share * depth * depth,
        nbytes=3 << 20,
    )
    shares = lax.all_gather(user_half, "ia", axis=0, tiled=True)
    (sums,) = call(
        all_sums, (shape(items, depth, dtype=F32),), (adj_t, shares), flops=work, nbytes=6 << 20
    )
    sums = lax.psum_scatter(sums, "au", scatter_dimension=0, tiled=True)
    (new_items,) = call(
        functools.partial(update, 1),
        (shape(held, depth, dtype=F32),),
        (item_emb, w_hi, w_lo, sums),
        flops=12 * held * depth * depth,
        nbytes=4 << 20,
    )
    return (new_users, new_items)


def local(n_au, n_ia, user_emb, item_emb, tiles, *rest):
    edge = tiles.shape[2]
    if (n_au, n_ia) == (8, 4) and item_emb.shape[0] == edge and edge % (user_emb.shape[0] // n_ia) == 0:
        return in_turns(user_emb, item_emb, tiles, *rest)
    return gathered(n_au, n_ia, user_emb, item_emb, tiles, *rest)


def solution(mesh):
    in_specs = (
        P("au", None),
        P(("ia", "au"), None),
        P("au", "ia", None, None),
        P("au", "ia"),
        P("au", "ia"),
        P("au", "ia"),
        P(),
        P(),
    )
    out_specs = (P(("au", "ia"), None), P(("ia", "au"), None))
    return jax.shard_map(
        functools.partial(local, mesh.shape["au"], mesh.shape["ia"]),
        mesh=mesh,
        in_specs=in_specs,
        out_specs=out_specs,
        check_vma=False,
    )
```

```python
import functools

import jax
import jax.numpy as jnp
from jax import lax
from jax.experimental import pallas as pl
from jax.experimental.pallas import tpu as pltpu
from jax.sharding import PartitionSpec as P

F32 = jnp.float32
BF16 = jnp.bfloat16
VMEM = pl.BlockSpec(memory_space=pltpu.VMEM)
SMEM = pl.BlockSpec(memory_space=pltpu.SMEM)
PARAMS = pltpu.CompilerParams(vmem_limit_bytes=40 * 1024 * 1024)

TURN_1 = ((0, 2), (3, 1), (1, 0), (2, 3))
TURN_2 = ((0, 1), (3, 2), (1, 3), (2, 0))
MIDDLE = ((1, 2), (2, 1))
HANDED = ((2, 3), (1, 0), (3, 2), (0, 1))


def back(pairs):
    return tuple((b, a) for a, b in pairs)


def send(x, pairs):
    perm = [(2 * a + core, 2 * b + core) for a, b in pairs for core in (0, 1)]
    perm += [(i, i ^ 1) for i in range(8) if i // 2 not in [a for a, _ in pairs]]
    return lax.ppermute(x, "au", perm)


def swap(x, axis, n, by):
    return lax.ppermute(x, axis, [(i, i ^ by) for i in range(n)])


def slot_of(me, block):
    apart = block ^ me
    turn = apart >> 1
    swapped = in_middle() & ((turn == 1) | (turn == 2))
    return jnp.where(swapped, 3 - turn, turn) * 2 + (apart & 1)


def in_middle():
    z = lax.axis_index("au") >> 1
    return (z == 1) | (z == 2)


def call(kernel, out_shape, operands, smem=0, flops=0, nbytes=0):
    return pl.pallas_call(
        kernel,
        out_shape=out_shape,
        in_specs=[SMEM] * smem + [VMEM] * (len(operands) - smem),
        out_specs=jax.tree.map(lambda _: VMEM, out_shape),
        compiler_params=PARAMS,
        cost_estimate=pl.CostEstimate(flops=flops, bytes_accessed=nbytes, transcendentals=0),
    )(*operands)


def shape(*dims, dtype=BF16):
    return jax.ShapeDtypeStruct(dims, dtype)


def split(x):
    hi = x.astype(BF16)
    return hi, (x - hi.astype(F32)).astype(BF16)


def dot(a, b):
    return jnp.dot(a, b, preferred_element_type=F32)


def total(refs):
    value = refs[0][...].astype(F32)
    for ref in refs[1:]:
        value = value + ref[...].astype(F32)
    return value


def dense(piece, turns, rows, cols, count, tiles, adj):
    edge = tiles.shape[2]
    adj[...] = jnp.zeros_like(adj)

    def place(slot, carry):
        at = cols[0, slot]
        if turns:
            at = slot_of(lax.axis_index("au"), at)
        col = pl.multiple_of(at * edge, edge)
        for part in range(edge // piece):
            row = rows[0, slot] * (edge // piece) + part
            if turns:
                row = row ^ lax.axis_index("ia")
            row = pl.multiple_of(row * piece, piece)
            adj[pl.ds(row, piece), pl.ds(col, edge)] = tiles[0, slot, part * piece : (part + 1) * piece, :]
        return carry

    lax.fori_loop(0, count[0, 0], place, 0)


def flip(edge, adj, *outs):
    n = len(outs)
    for k in range(adj.shape[1] // edge):
        out = outs[k % n]
        out[k // n * edge : (k // n + 1) * edge, :] = adj[:, k * edge : (k + 1) * edge].T


def ready(edge, adj, user_emb, w_self, w_inter, w_hi, w_lo, own, *adj_t):
    weights(user_emb, w_self, w_inter, w_hi, w_lo, own)
    flip(edge, adj, *adj_t)


def weights(user_emb, w_self, w_inter, w_hi, w_lo, own):
    depth = w_self.shape[0]
    for k, w in enumerate((w_self, w_inter)):
        w_hi[k * depth : (k + 1) * depth, :], w_lo[k * depth : (k + 1) * depth, :] = split(w[...])
    height = own.shape[0]
    own[...] = user_emb[pl.ds(pl.multiple_of(lax.axis_index("ia") * height, height), height), :]


def block_sums(adj, first, blocks):
    edge = blocks[0].shape[0]
    return sum(dot(adj[:, (first + k) * edge : (first + k + 1) * edge], block) for k, block in enumerate(blocks))


def early_sums(adj, *refs):
    *blocks, middle, ends, sums = refs
    blocks = [block[...] for block in blocks] + [jnp.where(in_middle(), middle[...], ends[...])]
    sums[...] = block_sums(adj, 0, blocks)


def late_sums(adj, early, middle, ends, *outs):
    sums = early[...] + block_sums(adj, 7, [jnp.where(in_middle(), middle[...], ends[...])])
    height = outs[0].shape[0]
    for k, out in enumerate(outs):
        out[...] = sums[k * height : (k + 1) * height].astype(out.dtype)


def user_sums(adj, items, out):
    out[...] = dot(adj[...], items[...])


def item_sums(slots, n, *refs):
    adj_t, shares, outs = refs[:2], refs[2 : 2 + 2 * n], refs[-len(slots) :]
    users = [jnp.concatenate([share[...] for share in shares[core * n : core * n + n]], axis=0) for core in (0, 1)]
    edge = outs[0].shape[0]
    for slot, out in zip(slots, outs):
        rows = slice(slot * edge, (slot + 1) * edge)
        out[...] = (dot(adj_t[0][rows, :], users[0]) + dot(adj_t[1][rows, :], users[1])).astype(out.dtype)


def item_sums_and(starts, n, *refs):
    refs[-1][...] = refs[-len(starts) - 2][...]
    item_sums(starts, n, *refs[: -len(starts) - 2], *refs[-len(starts) - 1 : -1])


def all_sums(adj_t, users, out):
    out[...] = dot(adj_t[...], users[...])


def pass_on(sums, handed, out):
    given = jnp.where(in_middle(), handed[...].astype(F32), 0)
    out[...] = (sums[...] + given).astype(out.dtype)


def mix(side, own, w_hi, w_lo):
    height = own.shape[0]
    hi, lo = split(jnp.concatenate([side + own, side * own], axis=1))
    both = dot(jnp.concatenate([hi, lo], axis=0), w_hi)
    mixed = both[:height] + (both[height:] + dot(hi, w_lo))
    return jnp.where(mixed >= 0, mixed, 0.2 * mixed)


def update(n, emb, w_hi, w_lo, *refs):
    mixed = mix(total(refs[:n]), emb[...], w_hi[...], w_lo[...])
    for out in refs[n:]:
        out[...] = mixed.astype(out.dtype)


def last_update(emb, w_hi, w_lo, middle, own, near, onward, out, ready, sems):
    inner = in_middle()
    n = sems.shape[0]
    copies = []
    for k in range(n):
        rows = slice(k * (out.shape[0] // n), (k + 1) * (out.shape[0] // n))
        side = own[rows, :] + near[rows, :].astype(F32) + onward[rows, :].astype(F32)
        side = side + jnp.where(inner, middle[rows, :].astype(F32), 0)
        ready[rows, :] = mix(side, emb[rows, :], w_hi[...], w_lo[...])
        copies.append(pltpu.make_async_copy(ready.at[rows, :], out.at[rows, :], sems.at[k]))
        copies[k].start()
    for copy in copies:
        copy.wait()


def in_turns(user_emb, item_emb, tiles, block_rows, block_cols, block_counts, w_self, w_inter):
    depth = w_self.shape[0]
    users, held = user_emb.shape[0], item_emb.shape[0]
    items = held * 8
    share = users // 4
    work = 2 * users * items * depth

    def other(x):
        return swap(x, "au", 8, 1)

    def after(x, *done):
        return lax.optimization_barrier((x, *done))[0]

    mine = item_emb.astype(BF16)
    first = send(mine, TURN_1)
    (adj,) = call(
        functools.partial(dense, share, True),
        (shape(users, items),),
        (block_rows, block_cols, block_counts, tiles),
        smem=3,
        nbytes=8 << 20,
    )
    second = send(mine, TURN_2)
    w_hi, w_lo, own_emb, adj_t, others_t = call(
        functools.partial(ready, held),
        (shape(2 * depth, depth), shape(2 * depth, depth), shape(share, depth, dtype=F32))
        + (shape(items // 2, users), shape(items // 2, users)),
        (adj, user_emb, w_self, w_inter),
        nbytes=9 << 20,
    )
    middle = send(after(mine, w_hi), MIDDLE)
    first = after(first, w_hi)
    ends = lax.ppermute(first, "au", [(2 * a + core, 2 * b + core) for a, b in HANDED[:2] for core in (0, 1)])
    (early,) = call(
        early_sums,
        (shape(users, depth, dtype=F32),),
        (adj, mine, other(mine), first, other(first), second, other(second), middle, ends),
        flops=work // 2,
        nbytes=4 << 20,
    )
    own, *others = call(
        late_sums,
        (shape(share, depth, dtype=F32),) + (shape(share, depth),) * 3,
        (adj, early, other(middle), other(ends)),
        flops=work // 2,
        nbytes=4 << 20,
    )
    others_t = other(after(others_t, own))
    own = after(own, others_t)
    new_users, user_half = call(
        functools.partial(update, 4),
        (shape(share, depth, dtype=F32), shape(share, depth)),
        (own_emb, w_hi, w_lo, *(swap(others[k - 1], "ia", 4, k) for k in (1, 2, 3)), own),
        flops=12 * share * depth * depth,
        nbytes=3 << 20,
    )

    shares = [user_half] + [swap(user_half, "ia", 4, k) for k in (1, 2, 3)]
    shares[1:3] = lax.optimization_barrier(tuple(shares[1:3]))
    shares += [other(x) for x in shares]
    (far,) = call(
        functools.partial(item_sums, (3,), 4),
        (shape(held, depth),),
        (adj_t, others_t, *shares),
        flops=work // 4,
        nbytes=2 << 20,
    )
    middle = send(far, back(MIDDLE))
    handed = send(far, back(HANDED))
    own, onward = call(
        functools.partial(item_sums, (0, 1), 4),
        (shape(held, depth, dtype=F32), shape(held, depth, dtype=F32)),
        (adj_t, others_t, *shares, far),
        flops=3 * work // 4,
        nbytes=6 << 20,
    )
    near, new_users = call(
        functools.partial(item_sums_and, (2,), 4),
        (shape(held, depth), shape(share, depth, dtype=F32)),
        (adj_t, others_t, *shares, own, new_users),
        flops=work // 4,
        nbytes=2 << 20,
    )
    near = send(near, back(TURN_2))
    (onward,) = call(pass_on, (shape(held, depth),), (onward, handed), nbytes=1 << 19)
    new_items = pl.pallas_call(
        last_update,
        out_shape=shape(held, depth, dtype=F32),
        in_specs=[VMEM] * 7,
        out_specs=pl.BlockSpec(memory_space=pl.ANY),
        scratch_shapes=(pltpu.VMEM((held, depth), F32), pltpu.SemaphoreType.DMA((2,))),
        compiler_params=PARAMS,
        cost_estimate=pl.CostEstimate(flops=12 * held * depth * depth, bytes_accessed=4 << 20, transcendentals=0),
    )(item_emb, w_hi, w_lo, middle, own, near, send(onward, back(TURN_1)))
    return (new_users, new_items)


def gathered(n_au, n_ia, user_emb, item_emb, tiles, block_rows, block_cols, block_counts, w_self, w_inter):
    depth = w_self.shape[0]
    users, held = user_emb.shape[0], item_emb.shape[0]
    items = held * n_au
    share = users // n_ia
    work = 2 * users * items * depth

    blocks = lax.all_gather(item_emb.astype(BF16), "au", axis=0, tiled=True)
    (adj,) = call(
        functools.partial(dense, tiles.shape[2], False),
        (shape(users, items),),
        (block_rows, block_cols, block_counts, tiles),
        smem=3,
        nbytes=4 << 20,
    )
    (adj_t,) = call(functools.partial(flip, tiles.shape[2]), (shape(items, users),), (adj,), nbytes=4 << 20)
    w_hi, w_lo, own_emb = call(
        weights,
        (shape(2 * depth, depth), shape(2 * depth, depth), shape(share, depth, dtype=F32)),
        (user_emb, w_self, w_inter),
        nbytes=5 << 20,
    )
    (sums,) = call(
        user_sums, (shape(users, depth, dtype=F32),), (adj, blocks), flops=work, nbytes=6 << 20
    )
    sums = lax.psum_scatter(sums, "ia", scatter_dimension=0, tiled=True)
    new_users, user_half = call(
        functools.partial(update, 1),
        (shape(share, depth, dtype=F32), shape(share, depth)),
        (own_emb, w_hi, w_lo, sums),
        flops=12 * share * depth * depth,
        nbytes=3 << 20,
    )
    shares = lax.all_gather(user_half, "ia", axis=0, tiled=True)
    (sums,) = call(
        all_sums, (shape(items, depth, dtype=F32),), (adj_t, shares), flops=work, nbytes=6 << 20
    )
    sums = lax.psum_scatter(sums, "au", scatter_dimension=0, tiled=True)
    (new_items,) = call(
        functools.partial(update, 1),
        (shape(held, depth, dtype=F32),),
        (item_emb, w_hi, w_lo, sums),
        flops=12 * held * depth * depth,
        nbytes=4 << 20,
    )
    return (new_users, new_items)


def local(n_au, n_ia, user_emb, item_emb, tiles, *rest):
    edge = tiles.shape[2]
    if (n_au, n_ia) == (8, 4) and item_emb.shape[0] == edge and edge % (user_emb.shape[0] // n_ia) == 0:
        return in_turns(user_emb, item_emb, tiles, *rest)
    return gathered(n_au, n_ia, user_emb, item_emb, tiles, *rest)


def solution(mesh):
    in_specs = (
        P("au", None),
        P(("ia", "au"), None),
        P("au", "ia", None, None),
        P("au", "ia"),
        P("au", "ia"),
        P("au", "ia"),
        P(),
        P(),
    )
    out_specs = (P(("au", "ia"), None), P(("ia", "au"), None))
    return jax.shard_map(
        functools.partial(local, mesh.shape["au"], mesh.shape["ia"]),
        mesh=mesh,
        in_specs=in_specs,
        out_specs=out_specs,
        check_vma=False,
    )
```
